256 devices in a mesh: slab: 128 (over z_lo, x, y, core), row: 2 (over z_hi).
Axes of the slice: x: 4, y: 4, z: 8 (z_hi: 2, z_lo: 4; z = z_hi * 4 + z_lo), core: 2. Of those that a mesh axis runs over, the one named last changes fastest.
Arguments:
- start_block: float32 [64, 524288], P(None, ('slab', 'row')), may hold values from -960 to 960
- prior_direction: float32 [64, 524288], P(None, ('slab', 'row')), may hold values from -480 to 480
- col_index: int32 [4096, 3], P(('slab', 'row')), may hold values from 0 to 4095, as said below
- k_blocks: float32 [4096, 3, 128, 128], P(('slab', 'row')), may hold values from -1 to 1
- m_blocks: float32 [4096, 3, 128, 128], P(('slab', 'row')), may hold values from -1 to 1
- k_diagonal: float32 [524288], P(('slab', 'row')), may hold values from 2 to 8
- m_diagonal: float32 [524288], P(('slab', 'row')), may hold values from 1 to 4
Outputs:
- iterate: float32 [64, 524288], P(None, ('slab', 'row'))
- prior: float32 [64, 524288], P(None, ('slab', 'row'))
The draws below stay inside these ranges and needn't reach their ends.
Inputs may be any that keep to these rules, and one draw needn't show every extreme that they name: col_index[g, 0] = g; entries 1 and 2 of row g are block rows other than g within 2 of g (they may be equal); col_index[g, j] = h for j >= 1 exactly when col_index[h, j] = g.
All inputs are finite; a program needn't handle non-finite values.
Results may differ from the reference program's by a relative error of at most 0.0003.
Values sent between devices are 32-bit elements; how exact they have to be, the bound alone decides.
No kernel may reach another device: no remote copies, remote signals or barrier semaphores. Data moves between devices by JAX's collectives and lax.ppermute only.
A program may use at most 64 MiB of HBM per device.

```python
import math
import jax
import jax.numpy as jnp
from jax import lax

COLS = 64
BS = 128
NNZ = 3
BLK_DEV = 16
ITERS = 2
BLOCKS = 4096
ROWS = 524288


def heavy_window(key):
    window_key = jax.random.fold_in(key, 7)
    span = BLK_DEV * BS
    owners = ROWS // span
    chosen = jax.random.randint(window_key, (), 0, owners, jnp.int32)
    owner_of = jnp.arange(ROWS, dtype=jnp.int32) // span
    return jnp.where(owner_of == chosen, 8.0, 1.0).astype(jnp.float32)


def row_scales(key, rise):
    position = jnp.arange(ROWS, dtype=jnp.float32) / ROWS
    rough = jnp.exp(jax.random.uniform(key, (ROWS,), jnp.float32) * math.log(10.0))
    return (1.0 + rise * position) * rough


def draw_start_block(key, part):
    heavy = heavy_window(key)
    key = jax.random.fold_in(key, 21)
    core_key, scale_key = jax.random.split(key)
    core = jax.random.truncated_normal(core_key, -4.0, 4.0, (COLS, ROWS), jnp.float32)
    return core * (row_scales(scale_key, 2.0) * heavy)[None, :]


def draw_prior_direction(key, part):
    heavy = heavy_window(key)
    key = jax.random.fold_in(key, 37)
    core_key, scale_key = jax.random.split(key)
    core = jax.random.truncated_normal(core_key, -4.0, 4.0, (COLS, ROWS), jnp.float32)
    return 0.5 * core * (row_scales(scale_key, 2.0) * heavy)[None, :]


def coupling(key):
    key = jax.random.fold_in(key, 53)
    first_key, second_key = jax.random.split(key)
    own_rows = jnp.arange(BLOCKS, dtype=jnp.int32)
    groups = BLOCKS // 4
    position_in = own_rows % 4
    first_pick = jax.random.randint(first_key, (groups,), 0, 2, jnp.int32)[own_rows // 4]
    across = jnp.where(position_in < 2, own_rows + 2, own_rows - 2)
    first_match = jnp.where(first_pick == 1, across, own_rows ^ 1)
    shifted = own_rows - 2
    shifted_in = shifted % 4
    shifted_group = jnp.clip(shifted // 4, 0, groups - 1)
    second_pick = jax.random.randint(second_key, (groups,), 0, 2, jnp.int32)[shifted_group]
    shifted_across = jnp.where(shifted_in < 2, own_rows + 2, own_rows - 2)
    inner_match = jnp.where(second_pick == 1, shifted_across, (shifted ^ 1) + 2)
    at_edge = (own_rows < 2) | (own_rows >= BLOCKS - 2)
    second_match = jnp.where(at_edge, own_rows ^ 1, inner_match)
    return jnp.stack([own_rows, first_match, second_match], 1).astype(jnp.int32)


def symmetric_blocks(key, values_key, spread_scale):
    pattern = coupling(key)
    raw_blocks = jax.random.truncated_normal(values_key, -4.0, 4.0, (BLOCKS, NNZ, BS, BS), jnp.float32) * (spread_scale / math.sqrt(BS))
    own_rows = jnp.arange(BLOCKS, dtype=jnp.int32)
    pieces = [0.5 * (raw_blocks[:, 0] + jnp.swapaxes(raw_blocks[:, 0], -1, -2))]
    for slot_no in (1, 2):
        partner = pattern[:, slot_no]
        mirrored = jnp.swapaxes(raw_blocks[partner, slot_no], -1, -2)
        pieces.append(jnp.where((own_rows < partner)[:, None, None], raw_blocks[:, slot_no], mirrored))
    return jnp.stack(pieces, 1)


def draw_col_index(key, part):
    return coupling(key)


def draw_k_blocks(key, part):
    values_key = jax.random.fold_in(key, 71)
    return symmetric_blocks(key, values_key, 0.25)


def draw_m_blocks(key, part):
    values_key = jax.random.fold_in(key, 89)
    return symmetric_blocks(key, values_key, 0.12)


def shard_levels(stream_key, dims, shards, low, largest):
    def one(axis_at, blocks):
        draws = jax.random.uniform(jax.random.fold_in(jax.random.fold_in(stream_key, 6), axis_at), (blocks,), jnp.float32, low / len(shards), largest / len(shards))
        return jnp.repeat(jnp.exp(draws), dims[axis_at] // blocks).reshape((-1,) + (1,) * (len(dims) - axis_at - 1))

    factor_of = one(*shards[0])
    for cut in shards[1:]:
        factor_of = factor_of * one(*cut)
    return factor_of


def setup_inputs(seed: int = 0) -> dict:
    keys = jax.random.split(jax.random.key(seed), 8)
    return {
        "start_block": draw_start_block(jax.random.fold_in(keys[7], 71), 0),
        "prior_direction": draw_prior_direction(jax.random.fold_in(keys[7], 71), 0),
        "col_index": draw_col_index(jax.random.fold_in(keys[7], 71), 0),
        "k_blocks": draw_k_blocks(jax.random.fold_in(keys[7], 71), 0),
        "m_blocks": draw_m_blocks(jax.random.fold_in(keys[7], 71), 0),
        "k_diagonal": jnp.clip(jnp.exp(math.log(8.0) - 1.3862944 * jax.random.uniform(keys[5], (ROWS,), jnp.float32) ** shard_levels(keys[5], (ROWS,), ((0, 256),), -0.2, 0.2)), 2.0, 8.0),
        "m_diagonal": jnp.clip(jnp.exp(math.log(4.0) - 1.3862944 * jax.random.uniform(keys[6], (ROWS,), jnp.float32) ** shard_levels(keys[6], (ROWS,), ((0, 256),), -0.2, 0.2)), 1.0, 4.0),
    }


HIGHEST = lax.Precision.HIGHEST

def symmetric(matrix):
    return 0.5 * (matrix + matrix.T)

def cross_gram(first_set, second_set):
    return jnp.einsum('ar,br->ab', first_set, second_set, precision=HIGHEST)

def combine(coeffs, basis):
    return jnp.einsum('ab,ar->br', coeffs, basis, precision=HIGHEST)

def multiply(left, right):
    return jnp.dot(left.astype(jnp.float32), right.astype(jnp.float32), precision=HIGHEST, preferred_element_type=jnp.float32)

def spd_solve(factor, right_side):
    half = lax.linalg.triangular_solve(factor, right_side, left_side=True, lower=True)
    return lax.linalg.triangular_solve(factor, half, left_side=True, lower=True, transpose_a=True)

def images(vectors, col_index, k_blocks, m_blocks, k_diagonal, m_diagonal):
    columns = vectors.shape[0]
    blocked = vectors.reshape(columns, -1, BS)
    k_image = k_diagonal[None, :] * vectors
    m_image = m_diagonal[None, :] * vectors
    for entry in range(NNZ):
        picked = blocked[:, col_index[:, entry]]
        k_image = k_image + jnp.einsum('gpq,cgq->cgp', k_blocks[:, entry], picked, precision=HIGHEST).reshape(columns, -1)
        m_image = m_image + jnp.einsum('gpq,cgq->cgp', m_blocks[:, entry], picked, precision=HIGHEST).reshape(columns, -1)
    return (k_image, m_image)

def reference(start_block, prior_direction, col_index, k_blocks, m_blocks, k_diagonal, m_diagonal):
    iterate = start_block
    prior = prior_direction
    k_both, m_both = images(jnp.concatenate([iterate, prior], 0), col_index, k_blocks, m_blocks, k_diagonal, m_diagonal)
    k_iter, k_prior = (k_both[:COLS], k_both[COLS:])
    m_iter, m_prior = (m_both[:COLS], m_both[COLS:])
    total_rows = iterate.shape[1]
    for iteration in range(ITERS):
        gram_x = symmetric(cross_gram(iterate, m_iter))
        ritz_x = symmetric(cross_gram(iterate, k_iter))
        ritz_matrix = spd_solve(jnp.linalg.cholesky(gram_x), ritz_x)
        search = (k_iter - combine(ritz_matrix, m_iter)) / k_diagonal[None, :]
        k_search, m_search = images(search, col_index, k_blocks, m_blocks, k_diagonal, m_diagonal)
        basis = jnp.concatenate([iterate, search, prior], 0)
        k_basis = jnp.concatenate([k_iter, k_search, k_prior], 0)
        m_basis = jnp.concatenate([m_iter, m_search, m_prior], 0)
        gram_k = symmetric(cross_gram(basis, k_basis))
        gram_m = symmetric(cross_gram(basis, m_basis))
        coeffs = spd_solve(jnp.linalg.cholesky(gram_k), gram_m[:, :COLS])
        trial = combine(coeffs, basis)
        m_trial = combine(coeffs, m_basis)
        norm_gram = symmetric(cross_gram(trial, m_trial))
        norm_factor = jnp.linalg.cholesky(norm_gram / total_rows)
        inverse_t = lax.linalg.triangular_solve(norm_factor, jnp.eye(COLS, dtype=jnp.float32), left_side=True, lower=True, transpose_a=True)
        mixing = multiply(coeffs, inverse_t)
        iterate = combine(mixing, basis)
        k_iter = combine(mixing, k_basis)
        m_iter = combine(mixing, m_basis)
        prior = combine(mixing[COLS:], basis[COLS:])
        k_prior = combine(mixing[COLS:], k_basis[COLS:])
        m_prior = combine(mixing[COLS:], m_basis[COLS:])
    return (iterate, prior)
```

```python
import jax
import jax.numpy as jnp
from jax import lax
from jax.experimental import pallas as pl
from jax.experimental.pallas import tpu as pltpu
from jax.sharding import PartitionSpec as P

COLS = 64
BS = 128
FACE = 2
NNZ = 3
AXES = ("slab", "row")
HIGHEST = lax.Precision.HIGHEST
STEP = 4
VMEM_LIMIT = 48 * 1024 * 1024


def coords(i):
    zh, c, y, x, zl = i & 1, (i >> 1) & 1, (i >> 2) & 3, (i >> 4) & 3, (i >> 6) & 3
    return {"x": x, "y": y, "z": zh * 4 + zl, "c": c}


def flat(d):
    zh, zl = d["z"] >> 2, d["z"] & 3
    return (((zl * 4 + d["x"]) * 4 + d["y"]) * 2 + d["c"]) * 2 + zh


def partner(x, axis, k):
    pairs = []
    for i in range(256):
        d = coords(i)
        d[axis] ^= k
        pairs.append((i, flat(d)))
    return lax.ppermute(x, AXES, pairs)


def all_sum(x):
    for axis, ks in (("c", (1,)), ("x", (1, 2, 3)), ("y", (1, 2, 3)), ("z", (1, 2, 3)), ("z", (4,))):
        parts = [partner(x, axis, k) for k in ks]
        for part in parts:
            x = x + part
    return x


def halo(head, tail):
    count = lax.axis_size("slab") * lax.axis_size("row")
    forward = [(i, i + 1) for i in range(count - 1)]
    backward = [(i + 1, i) for i in range(count - 1)]
    return lax.ppermute(tail, AXES, forward), lax.ppermute(head, AXES, backward)


def split(x):
    hi = x.astype(jnp.bfloat16)
    return hi, (x - hi.astype(jnp.float32)).astype(jnp.bfloat16)


def dot3(a, b, dims):
    def dot(u, v):
        return lax.dot_general(u, v, (dims, ((), ())), preferred_element_type=jnp.float32)

    return dot(a[0], b[0]) + (dot(a[0], b[1]) + dot(a[1], b[0]))


NT = ((1,), (1,))
TN = ((0,), (0,))
NN = ((1,), (0,))


def exact(a, b, dims=NN):
    return lax.dot_general(a, b, (dims, ((), ())), precision=HIGHEST, preferred_element_type=jnp.float32)


def sym(a):
    return 0.5 * (a + a.T)


def factor_inverses(mats):
    rows = lax.broadcasted_iota(jnp.int32, (COLS, 1), 0)
    eye = (
        lax.broadcasted_iota(jnp.int32, (COLS, COLS), 0) == lax.broadcasted_iota(jnp.int32, (COLS, COLS), 1)
    ).astype(jnp.float32)
    work = [jnp.concatenate([a, eye], 1) for a in mats]
    for j in range(COLS - 1):
        for n, w in enumerate(work):
            row = w[j : j + 1, :]
            scaled = row * (1.0 / w[j : j + 1, j : j + 1])
            col = jnp.where(rows > j, w[:, j : j + 1], 0.0)
            work[n] = w - col * scaled
    out = []
    for w in work:
        d = jnp.sum(w[:, :COLS] * eye, axis=1, keepdims=True)
        r = lax.rsqrt(d)
        r = r * (1.5 - 0.5 * d * r * r)
        out.append(w[:, COLS:] * r)
    return out


def chain(first, second, total_rows):
    xx_k, xx_m = sym(first[0:64, 0:64]), sym(first[0:64, 64:128])
    px_k, px_m = first[64:128, 0:64], first[64:128, 64:128]
    pp_k, pp_m = sym(first[128:192, 0:64]), sym(first[128:192, 64:128])
    sx_k, sp_k = second[0:64, 0:64], second[0:64, 64:128]
    sx_m, sp_m = second[64:128, 0:64], second[64:128, 64:128]
    ss_k, ss_m = sym(second[128:192, 0:64]), sym(second[128:192, 64:128])
    (l1,) = factor_inverses([xx_k])
    y1 = exact(l1, xx_m)
    l21 = exact(px_k, l1, NT)
    l31 = exact(sx_k, l1, NT)
    (l2,) = factor_inverses([pp_k - exact(l21, l21, NT)])
    l32 = exact(sp_k - exact(l31, l21, NT), l2, NT)
    y2 = exact(l2, px_m - exact(l21, y1))
    (l3,) = factor_inverses([ss_k - exact(l31, l31, NT) - exact(l32, l32, NT)])
    y3 = exact(l3, sx_m - exact(l31, y1) - exact(l32, y2))
    z3 = exact(l3, y3, TN)
    z2 = exact(l2, y2 - exact(l32, z3, TN), TN)
    z1 = exact(l1, y1 - exact(l21, z2, TN) - exact(l31, z3, TN), TN)
    gram_k = jnp.concatenate(
        [
            jnp.concatenate([xx_k, px_k.T, sx_k.T], 1),
            jnp.concatenate([px_k, pp_k, sp_k.T], 1),
            jnp.concatenate([sx_k, sp_k, ss_k], 1),
        ],
        0,
    )
    gram_m = jnp.concatenate(
        [
            jnp.concatenate([xx_m, px_m.T, sx_m.T], 1),
            jnp.concatenate([px_m, pp_m, sp_m.T], 1),
            jnp.concatenate([sx_m, sp_m, ss_m], 1),
        ],
        0,
    )
    coeffs = jnp.concatenate([z1, z2, z3], 0)
    norm = sym(exact(coeffs, exact(gram_m, coeffs), TN))
    (ln,) = factor_inverses([norm * (1.0 / total_rows)])
    return exact(coeffs, ln, NT), gram_k, gram_m


def both(mixing):
    return jnp.concatenate([mixing, jnp.concatenate([jnp.zeros((64, 64), jnp.float32), mixing[64:]], 0)], 1)


def block_row(t, g, col_ref, k_ref, m_ref, hi_ref, lo_ref):
    acc = None
    for j in range(NNZ):
        at = col_ref[g, j]
        w = split(jnp.concatenate([k_ref[t, j], m_ref[t, j]], 0))
        term = dot3((hi_ref[at], lo_ref[at]), w, NT)
        acc = term if acc is None else acc + term
    return acc


def first_kernel(
    col_ref, x_ref, p_ref, low_ref, high_ref, k_ref, m_ref, kd_ref, md_ref, kv_ref, mv_ref, gram_ref, hi_ref, lo_ref, acc_ref
):
    i = pl.program_id(0)
    blocks = x_ref.shape[1] // BS

    @pl.when(i == 0)
    def _():
        acc_ref[...] = jnp.zeros_like(acc_ref)
        for b in range(FACE):
            hi_ref[b], lo_ref[b] = split(low_ref[0:128, b * BS : (b + 1) * BS])
            hi_ref[b + FACE + blocks], lo_ref[b + FACE + blocks] = split(high_ref[0:128, b * BS : (b + 1) * BS])
        for b in range(blocks):
            tile = jnp.concatenate([x_ref[:, b * BS : (b + 1) * BS], p_ref[:, b * BS : (b + 1) * BS]], 0)
            hi_ref[b + FACE], lo_ref[b + FACE] = split(tile)

    for t in range(STEP):
        g = i * STEP + t
        here = pl.ds(pl.multiple_of(g * BS, BS), BS)
        acc = block_row(t, g, col_ref, k_ref, m_ref, hi_ref, lo_ref)
        tile = jnp.concatenate([x_ref[:, here], p_ref[:, here]], 0)
        kv = acc[:, :BS] + kd_ref[:, here] * tile
        mv = acc[:, BS:] + md_ref[:, here] * tile
        kv_ref[:, t * BS : (t + 1) * BS] = kv
        mv_ref[:, t * BS : (t + 1) * BS] = mv
        acc_ref[...] += dot3(split(jnp.concatenate([kv, mv], 0)), (hi_ref[g + FACE], lo_ref[g + FACE]), NT)

    @pl.when(i == pl.num_programs(0) - 1)
    def _():
        gram = acc_ref[...]
        gram_ref[0:64] = jnp.concatenate([gram[0:64, 0:64], gram[128:192, 0:64]], 1)
        gram_ref[64:128] = jnp.concatenate([gram[64:128, 0:64], gram[192:256, 0:64]], 1)
        gram_ref[128:192] = jnp.concatenate([gram[64:128, 64:128], gram[192:256, 64:128]], 1)


def search_blocks(s_ref, hi_ref, lo_ref, low, high, mine):
    blocks = s_ref.shape[1] // BS
    for b in range(FACE):
        hi_ref[b], lo_ref[b] = split(low[:, b * BS : (b + 1) * BS])
        hi_ref[b + FACE + blocks], lo_ref[b + FACE + blocks] = split(high[:, b * BS : (b + 1) * BS])
    for b in range(0, blocks, STEP):
        s = mine(slice(b * BS, (b + STEP) * BS))
        s_ref[:, b * BS : (b + STEP) * BS] = s
        for t in range(STEP):
            hi_ref[b + t + FACE], lo_ref[b + t + FACE] = split(s[:, t * BS : (t + 1) * BS])


def search_steps(i, col_ref, x_ref, p_ref, s_ref, k_ref, m_ref, kd_ref, md_ref, ks_ref, ms_ref, gram_ref, hi_ref, lo_ref, acc_ref):
    for t in range(STEP):
        g = i * STEP + t
        here = pl.ds(pl.multiple_of(g * BS, BS), BS)
        acc = block_row(t, g, col_ref, k_ref, m_ref, hi_ref, lo_ref)
        s = s_ref[:, here]
        ks = acc[:, :BS] + kd_ref[:, here] * s
        ms = acc[:, BS:] + md_ref[:, here] * s
        if ks_ref is not None:
            ks_ref[:, t * BS : (t + 1) * BS] = ks
            ms_ref[:, t * BS : (t + 1) * BS] = ms
        basis = split(jnp.concatenate([x_ref[:, here], p_ref[:, here]], 0))
        basis = tuple(jnp.concatenate([u, v[g + FACE]], 0) for u, v in zip(basis, (hi_ref, lo_ref)))
        acc_ref[...] += dot3(split(jnp.concatenate([ks, ms], 0)), basis, NT)

    @pl.when(i == pl.num_programs(0) - 1)
    def _():
        gram = acc_ref[...]
        gram_ref[0:128] = gram[:, 0:128]
        gram_ref[128:192] = jnp.concatenate([gram[0:64, 128:192], gram[64:128, 128:192]], 1)


def second_kernel(
    col_ref, first_ref, x_ref, p_ref, kv_ref, mv_ref, low_ref, high_ref, kdl_ref, kdh_ref, k_ref, m_ref, kd_ref, md_ref,
    s_ref, ks_ref, ms_ref, gram_ref, hi_ref, lo_ref, acc_ref,
):
    i = pl.program_id(0)

    @pl.when(i == 0)
    def _():
        acc_ref[...] = jnp.zeros_like(acc_ref)
        (inv,) = factor_inverses([sym(first_ref[0:64, 64:128])])
        ritz = split(exact(inv, exact(inv, sym(first_ref[0:64, 0:64])), TN))

        def search(kx, mx, kd):
            return (kx - dot3(ritz, split(mx), TN)) / kd

        search_blocks(
            s_ref, hi_ref, lo_ref,
            search(low_ref[0:64], low_ref[64:128], kdl_ref[0:1]),
            search(high_ref[0:64], high_ref[64:128], kdh_ref[0:1]),
            lambda at: search(kv_ref[0:64, at], mv_ref[0:64, at], kd_ref[:, at]),
        )

    search_steps(i, col_ref, x_ref, p_ref, s_ref, k_ref, m_ref, kd_ref, md_ref, ks_ref, ms_ref, gram_ref, hi_ref, lo_ref, acc_ref)


def third_kernel(
    total_rows,
    col_ref, first_ref, second_ref, x_ref, p_ref, s_ref, kv_ref, mv_ref, ks_ref, ms_ref,
    xlow_ref, xhigh_ref, slow_ref, shigh_ref, kdl_ref, kdh_ref, k_ref, m_ref, kd_ref, md_ref,
    xo_ref, po_ref, so_ref, firsto_ref, gram_ref, hi_ref, lo_ref, acc_ref,
):
    i = pl.program_id(0)

    @pl.when(i == 0)
    def _():
        acc_ref[...] = jnp.zeros_like(acc_ref)
        mixing, gram_k, gram_m = chain(first_ref[...], second_ref[...], total_rows)
        pair = both(mixing)
        next_k = exact(pair, exact(gram_k, pair), TN)
        next_m = exact(pair, exact(gram_m, pair), TN)
        firsto_ref[0:64] = jnp.concatenate([next_k[0:64, 0:64], next_m[0:64, 0:64]], 1)
        firsto_ref[64:128] = jnp.concatenate([next_k[64:128, 0:64], next_m[64:128, 0:64]], 1)
        firsto_ref[128:192] = jnp.concatenate([next_k[64:128, 64:128], next_m[64:128, 64:128]], 1)
        ritz = sym(next_k[0:64, 0:64]) * (1.0 / total_rows)
        weights = split(jnp.concatenate([mixing, -exact(mixing, ritz)], 0))
        pair = split(pair)

        def search(parts, kd):
            return dot3(weights, split(jnp.concatenate(parts, 0)), TN) / kd

        search_blocks(
            so_ref, hi_ref, lo_ref,
            search([xlow_ref[0:64], slow_ref[0:128], xlow_ref[64:128], slow_ref[128:256]], kdl_ref[0:1]),
            search([xhigh_ref[0:64], shigh_ref[0:128], xhigh_ref[64:128], shigh_ref[128:256]], kdh_ref[0:1]),
            lambda at: search([kv_ref[:, at], ks_ref[:, at], mv_ref[:, at], ms_ref[:, at]], kd_ref[:, at]),
        )
        for b in range(0, x_ref.shape[1], 512):
            at = slice(b, b + 512)
            new = dot3(pair, split(jnp.concatenate([x_ref[:, at], p_ref[:, at], s_ref[:, at]], 0)), TN)
            xo_ref[:, at] = new[0:64]
            po_ref[:, at] = new[64:128]

    search_steps(i, col_ref, xo_ref, po_ref, so_ref, k_ref, m_ref, kd_ref, md_ref, None, None, gram_ref, hi_ref, lo_ref, acc_ref)


def last_kernel(total_rows, first_ref, second_ref, x_ref, p_ref, s_ref, xo_ref, po_ref):
    mixing, _, _ = chain(first_ref[...], second_ref[...], total_rows)
    pair = split(both(mixing))
    for b in range(0, x_ref.shape[1], 512):
        at = slice(b, b + 512)
        new = dot3(pair, split(jnp.concatenate([x_ref[:, at], p_ref[:, at], s_ref[:, at]], 0)), TN)
        xo_ref[:, at] = new[0:64]
        po_ref[:, at] = new[64:128]


def whole():
    return pl.BlockSpec(memory_space=pltpu.VMEM)


def smem():
    return pl.BlockSpec(memory_space=pltpu.SMEM)


def stored():
    return pl.BlockSpec((STEP, NNZ, BS, BS), lambda i: (i, 0, 0, 0))


def columns(rows):
    return pl.BlockSpec((rows, STEP * BS), lambda i: (0, i))


def f32(*shape):
    return jax.ShapeDtypeStruct(shape, jnp.float32)


def params():
    return pltpu.CompilerParams(vmem_limit_bytes=VMEM_LIMIT)


def shards(start_block, prior_direction, col_index, k_blocks, m_blocks, k_diagonal, m_diagonal):
    block_count = col_index.shape[0]
    local_rows = start_block.shape[1]
    devices = lax.axis_size("slab") * lax.axis_size("row")
    total_rows = float(local_rows * devices)
    edge = FACE * BS
    first_block = (lax.axis_index("slab") * lax.axis_size("row") + lax.axis_index("row")) * block_count - FACE
    col = col_index - first_block
    kd, md = k_diagonal[None, :], m_diagonal[None, :]
    grid = (block_count // STEP,)
    extended = block_count + 2 * FACE

    def edges(*parts):
        return (
            jnp.concatenate([a[:, :edge] for a in parts], 0),
            jnp.concatenate([a[:, local_rows - edge :] for a in parts], 0),
        )

    kd8 = jnp.broadcast_to(kd, (8, local_rows))
    low, high = halo(*edges(start_block, prior_direction, kd8))
    kdl, kdh = low[128:136], high[128:136]

    kv, mv, gram = pl.pallas_call(
        first_kernel,
        grid=grid,
        in_specs=[smem()] + [whole()] * 4 + [stored()] * 2 + [whole()] * 2,
        out_specs=[columns(128), columns(128), whole()],
        out_shape=[f32(128, local_rows), f32(128, local_rows), f32(192, 128)],
        scratch_shapes=[pltpu.VMEM((extended, 128, BS), jnp.bfloat16)] * 2 + [pltpu.VMEM((256, 128), jnp.float32)],
        compiler_params=params(),
        name="first_images",
    )(col, start_block, prior_direction, low, high, k_blocks, m_blocks, kd, md)

    xlow, xhigh = halo(*edges(kv[:64], mv[:64]))
    first = all_sum(gram)

    s, ks, ms, gram = pl.pallas_call(
        second_kernel,
        grid=grid,
        in_specs=[smem()] + [whole()] * 9 + [stored()] * 2 + [whole()] * 2,
        out_specs=[whole(), columns(64), columns(64), whole()],
        out_shape=[f32(64, local_rows)] * 3 + [f32(192, 128)],
        scratch_shapes=[pltpu.VMEM((extended, 64, BS), jnp.bfloat16)] * 2 + [pltpu.VMEM((128, 192), jnp.float32)],
        compiler_params=params(),
        name="search_images",
    )(col, first, start_block, prior_direction, kv, mv, xlow, xhigh, kdl, kdh, k_blocks, m_blocks, kd, md)

    slow, shigh = halo(*edges(kv[64:], ks, mv[64:], ms))
    second = all_sum(gram)

    x, p, s, first, gram = pl.pallas_call(
        lambda *refs: third_kernel(total_rows, *refs),
        grid=grid,
        in_specs=[smem()] + [whole()] * 15 + [stored()] * 2 + [whole()] * 2,
        out_specs=[whole()] * 5,
        out_shape=[f32(64, local_rows)] * 3 + [f32(192, 128)] * 2,
        scratch_shapes=[pltpu.VMEM((extended, 64, BS), jnp.bfloat16)] * 2 + [pltpu.VMEM((128, 192), jnp.float32)],
        compiler_params=params(),
        name="mixed_images",
    )(
        col, first, second, start_block, prior_direction, s, kv, mv, ks, ms,
        xlow, xhigh, slow, shigh, kdl, kdh, k_blocks, m_blocks, kd, md,
    )

    second = all_sum(gram)

    iterate, prior = pl.pallas_call(
        lambda *refs: last_kernel(total_rows, *refs),
        in_specs=[whole()] * 5,
        out_specs=[whole()] * 2,
        out_shape=[f32(64, local_rows)] * 2,
        compiler_params=params(),
        name="last_mix",
    )(first, second, x, p, s)
    return (iterate, prior)


def solution(mesh):
    in_specs = (
        P(None, ("slab", "row")),
        P(None, ("slab", "row")),
        P(("slab", "row"), None),
        P(("slab", "row"), None, None, None),
        P(("slab", "row"), None, None, None),
        P(("slab", "row")),
        P(("slab", "row")),
    )
    out_specs = (P(None, ("slab", "row")), P(None, ("slab", "row")))
    return jax.shard_map(shards, mesh=mesh, in_specs=in_specs, out_specs=out_specs, check_vma=False)
```

```python
import jax
import jax.numpy as jnp
from jax import lax
from jax.experimental import pallas as pl
from jax.experimental.pallas import tpu as pltpu
from jax.sharding import PartitionSpec as P

COLS = 64
BS = 128
FACE = 2
NNZ = 3
AXES = ("slab", "row")
HIGHEST = lax.Precision.HIGHEST
STEP = 2
VMEM_LIMIT = 48 * 1024 * 1024


def coords(i):
    zh, c, y, x, zl = i & 1, (i >> 1) & 1, (i >> 2) & 3, (i >> 4) & 3, (i >> 6) & 3
    return {"x": x, "y": y, "z": zh * 4 + zl, "c": c}


def flat(d):
    zh, zl = d["z"] >> 2, d["z"] & 3
    return (((zl * 4 + d["x"]) * 4 + d["y"]) * 2 + d["c"]) * 2 + zh


def partner(x, axis, k):
    pairs = []
    for i in range(256):
        d = coords(i)
        d[axis] ^= k
        pairs.append((i, flat(d)))
    return lax.ppermute(x, AXES, pairs)


ROUNDS = (("c", (1,)), ("x", (1, 2, 3)), ("y", (1, 2, 3)), ("z", (1, 2, 3)), ("z", (4,)))


def all_sum(x, given=None, tasks=()):
    for n, (axis, ks) in enumerate(ROUNDS):
        busy = 0 < n <= len(tasks)
        if busy:
            x, given = lax.optimization_barrier((x, given))
            given = tasks[n - 1](*given)
        for part in [partner(x, axis, k) for k in ks]:
            x = x + part
        if busy:
            x, given = lax.optimization_barrier((x, given))
    return (x, given) if tasks else x


def exchange(edges, task=None):
    head, tail = edges
    count = lax.axis_size("slab") * lax.axis_size("row")
    low = lax.ppermute(tail, AXES, [(i, i + 1) for i in range(count - 1)])
    given = None
    if task is not None:
        head, given = lax.optimization_barrier((head, task()))
    return low, lax.ppermute(head, AXES, [(i + 1, i) for i in range(count - 1)]), given


def split(x):
    hi = x.astype(jnp.bfloat16)
    return hi, (x - hi.astype(jnp.float32)).astype(jnp.bfloat16)


def dot3(a, b, dims):
    def dot(u, v):
        return lax.dot_general(u, v, (dims, ((), ())), preferred_element_type=jnp.float32)

    return dot(a[0], b[0]) + (dot(a[0], b[1]) + dot(a[1], b[0]))


NT = ((1,), (1,))
TN = ((0,), (0,))
NN = ((1,), (0,))


def exact(a, b, dims=NN):
    return lax.dot_general(a, b, (dims, ((), ())), precision=HIGHEST, preferred_element_type=jnp.float32)


def sym(a):
    return 0.5 * (a + a.T)


def factor_inverses(mats):
    rows = lax.broadcasted_iota(jnp.int32, (COLS, 1), 0)
    eye = (
        lax.broadcasted_iota(jnp.int32, (COLS, COLS), 0) == lax.broadcasted_iota(jnp.int32, (COLS, COLS), 1)
    ).astype(jnp.float32)
    work = [jnp.concatenate([a, eye], 1) for a in mats]
    for j in range(0, COLS, 2):
        for n, w in enumerate(work):
            r1, r2 = w[j : j + 1, :], w[j + 1 : j + 2, :]
            a, b, c = r1[:, j : j + 1], r1[:, j + 1 : j + 2], r2[:, j + 1 : j + 2]
            scale = 1.0 / (a * c - b * b)
            u1, u2 = (c * r1 - b * r2) * scale, (a * r2 - b * r1) * scale
            below = w[:, j : j + 1] * u1 + w[:, j + 1 : j + 2] * u2
            work[n] = w - jnp.where(rows > j + 1, below, jnp.where(rows == j + 1, (b / a) * r1, 0.0))
    out = []
    for w in work:
        d = jnp.sum(w[:, :COLS] * eye, axis=1, keepdims=True)
        r = lax.rsqrt(d)
        r = r * (1.5 - 0.5 * d * r * r)
        out.append(w[:, COLS:] * r)
    return out


def first_parts(first):
    return (
        (sym(first[0:64, 0:64]), first[64:128, 0:64], sym(first[128:192, 0:64])),
        (sym(first[0:64, 64:128]), first[64:128, 64:128], sym(first[128:192, 64:128])),
    )


def halves(first, second):
    out = []
    for n, (xx, px, pp) in enumerate(first_parts(first)):
        sx, sp = second[64 * n : 64 * n + 64, 0:64], second[64 * n : 64 * n + 64, 64:128]
        ss = sym(second[128:192, 64 * n : 64 * n + 64])
        out.append(
            jnp.concatenate(
                [
                    jnp.concatenate([xx, px.T, sx.T], 1),
                    jnp.concatenate([px, pp, sp.T], 1),
                    jnp.concatenate([sx, sp, ss], 1),
                ],
                0,
            )
        )
    return out


def prepare(first, l1, out_ref):
    (_, px_k, pp_k), (xx_m, px_m, _) = first_parts(first)
    y1 = exact(l1, xx_m)
    l21 = exact(px_k, l1, NT)
    (l2,) = factor_inverses([pp_k - exact(l21, l21, NT)])
    y2 = exact(l2, px_m - exact(l21, y1))
    for n, part in enumerate((l1, l2, l21, y1, y2)):
        out_ref[64 * n : 64 * n + 64] = part


def chain(first, second, ready, total_rows):
    l1, l2, l21, y1, y2 = (ready[64 * n : 64 * n + 64] for n in range(5))
    gram_k, gram_m = halves(first, second)
    sx_k, sp_k, ss_k, sx_m = gram_k[128:, 0:64], gram_k[128:, 64:128], gram_k[128:, 128:], gram_m[128:, 0:64]
    l31 = exact(sx_k, l1, NT)
    l32 = exact(sp_k - exact(l31, l21, NT), l2, NT)
    (l3,) = factor_inverses([ss_k - exact(l31, l31, NT) - exact(l32, l32, NT)])
    z3 = exact(l3, exact(l3, sx_m - exact(l31, y1) - exact(l32, y2)), TN)
    z2 = exact(l2, y2 - exact(l32, z3, TN), TN)
    z1 = exact(l1, y1 - exact(l21, z2, TN) - exact(l31, z3, TN), TN)
    coeffs = jnp.concatenate([z1, z2, z3], 0)
    norm = sym(exact(coeffs, exact(gram_m, coeffs), TN))
    (ln,) = factor_inverses([norm * (1.0 / total_rows)])
    return exact(coeffs, ln, NT), gram_k, gram_m


def both(mixing):
    return jnp.concatenate([mixing, jnp.concatenate([jnp.zeros((64, 64), jnp.float32), mixing[64:]], 0)], 1)


def block_row(t, g, col_ref, k_ref, m_ref, hi_ref, lo_ref):
    acc = None
    for j in range(NNZ):
        at = col_ref[g, j]
        w = split(jnp.concatenate([k_ref[t, j], m_ref[t, j]], 0))
        term = dot3((hi_ref[at], lo_ref[at]), w, NT)
        acc = term if acc is None else acc + term
    return acc


def fill(hi_ref, lo_ref, at, tiles):
    for b in range(tiles.shape[1] // BS):
        hi_ref[at + b], lo_ref[at + b] = split(tiles[:, b * BS : (b + 1) * BS])


def pair_steps(first, col_ref, xp_ref, k_ref, m_ref, kd_ref, md_ref, kv_ref, mv_ref, hi_ref, lo_ref, acc_ref):
    for t in range(STEP):
        g = first + t
        at = slice(t * BS, (t + 1) * BS)
        acc = block_row(t, g, col_ref, k_ref, m_ref, hi_ref, lo_ref)
        tile = xp_ref[:, pl.ds(pl.multiple_of(g * BS, BS), BS)]
        kv = acc[:, :BS] + kd_ref[:, at] * tile
        mv = acc[:, BS:] + md_ref[:, at] * tile
        kv_ref[:, at] = kv
        mv_ref[:, at] = mv
        acc_ref[...] += dot3(split(jnp.concatenate([kv, mv], 0)), (hi_ref[g + FACE], lo_ref[g + FACE]), NT)


def pair_inner(col_ref, xp_ref, k_ref, m_ref, kd_ref, md_ref, kv_ref, mv_ref, acc_ref, hi_ref, lo_ref):
    i = pl.program_id(0)

    @pl.when(i == 0)
    def _():
        acc_ref[...] = jnp.zeros_like(acc_ref)
        fill(hi_ref, lo_ref, FACE, xp_ref[...])

    pair_steps(i * STEP + FACE, col_ref, xp_ref, k_ref, m_ref, kd_ref, md_ref, kv_ref, mv_ref, hi_ref, lo_ref, acc_ref)


def fill_edges(v_ref, low_ref, high_ref, hi_ref, lo_ref):
    rows = v_ref.shape[1]
    blocks = rows // BS
    fill(hi_ref, lo_ref, 0, low_ref[...])
    fill(hi_ref, lo_ref, FACE, v_ref[:, : 2 * FACE * BS])
    fill(hi_ref, lo_ref, blocks - FACE, v_ref[:, rows - 2 * FACE * BS :])
    fill(hi_ref, lo_ref, FACE + blocks, high_ref[...])
    return blocks


def pair_edges(
    col_ref, xp_ref, low_ref, high_ref, part_ref, kvin_ref, mvin_ref, k_ref, m_ref, kd_ref, md_ref,
    kv_ref, mv_ref, gram_ref, hi_ref, lo_ref, acc_ref,
):
    i = pl.program_id(0)

    @pl.when(i == 0)
    def _():
        acc_ref[...] = part_ref[...]
        fill_edges(xp_ref, low_ref, high_ref, hi_ref, lo_ref)

    first = i * (xp_ref.shape[1] // BS - FACE)
    pair_steps(first, col_ref, xp_ref, k_ref, m_ref, kd_ref, md_ref, kv_ref, mv_ref, hi_ref, lo_ref, acc_ref)

    @pl.when(i == pl.num_programs(0) - 1)
    def _():
        gram = acc_ref[...]
        gram_ref[0:64] = jnp.concatenate([gram[0:64, 0:64], gram[128:192, 0:64]], 1)
        gram_ref[64:128] = jnp.concatenate([gram[64:128, 0:64], gram[192:256, 0:64]], 1)
        gram_ref[128:192] = jnp.concatenate([gram[64:128, 64:128], gram[192:256, 64:128]], 1)


def first_search(first_ref, kv_ref, mv_ref, kd_ref, s_ref, inv_ref):
    (xx_k, _, _), (xx_m, _, _) = first_parts(first_ref[...])
    inv, inv_k = factor_inverses([xx_m, xx_k])
    inv_ref[...] = inv_k
    ritz = split(exact(inv, exact(inv, xx_k), TN))
    for b in range(0, s_ref.shape[1], 512):
        at = slice(b, b + 512)
        s_ref[:, at] = (kv_ref[0:64, at] - dot3(ritz, split(mv_ref[0:64, at]), TN)) / kd_ref[:, at]


def search_steps(first, col_ref, xp_ref, s_ref, k_ref, m_ref, kd_ref, md_ref, out, hi_ref, lo_ref, acc_ref):
    for t in range(STEP):
        g = first + t
        at = slice(t * BS, (t + 1) * BS)
        here = pl.ds(pl.multiple_of(g * BS, BS), BS)
        acc = block_row(t, g, col_ref, k_ref, m_ref, hi_ref, lo_ref)
        s = s_ref[:, here]
        ks = acc[:, :BS] + kd_ref[:, at] * s
        ms = acc[:, BS:] + md_ref[:, at] * s
        if out:
            out[0][:, at] = ks
            out[1][:, at] = ms
        basis = tuple(jnp.concatenate([u, v[g + FACE]], 0) for u, v in zip(split(xp_ref[:, here]), (hi_ref, lo_ref)))
        acc_ref[...] += dot3(split(jnp.concatenate([ks, ms], 0)), basis, NT)


def search_inner(keep, col_ref, xp_ref, s_ref, k_ref, m_ref, kd_ref, md_ref, *rest):
    *out, acc_ref, hi_ref, lo_ref = rest
    i = pl.program_id(0)

    @pl.when(i == 0)
    def _():
        acc_ref[...] = jnp.zeros_like(acc_ref)
        fill(hi_ref, lo_ref, FACE, s_ref[...])

    search_steps(i * STEP + FACE, col_ref, xp_ref, s_ref, k_ref, m_ref, kd_ref, md_ref, out, hi_ref, lo_ref, acc_ref)


def search_edges(keep, col_ref, xp_ref, s_ref, low_ref, high_ref, part_ref, *rest):
    k_ref, m_ref, kd_ref, md_ref, *out, gram_ref, hi_ref, lo_ref, acc_ref = rest[2:] if keep else rest
    i = pl.program_id(0)

    @pl.when(i == 0)
    def _():
        acc_ref[...] = part_ref[...]
        fill_edges(s_ref, low_ref, high_ref, hi_ref, lo_ref)

    first = i * (s_ref.shape[1] // BS - FACE)
    search_steps(first, col_ref, xp_ref, s_ref, k_ref, m_ref, kd_ref, md_ref, out, hi_ref, lo_ref, acc_ref)

    @pl.when(i == pl.num_programs(0) - 1)
    def _():
        gram = acc_ref[...]
        gram_ref[0:128] = gram[:, 0:128]
        gram_ref[128:192] = jnp.concatenate([gram[0:64, 128:192], gram[64:128, 128:192]], 1)


def factor_pair(first_ref, inv_ref, ready_ref):
    prepare(first_ref[...], inv_ref[...], ready_ref)


def next_first(first_ref, second_ref, pair_ref, firsto_ref, inv_ref):
    pair = pair_ref[...]
    gram_k, gram_m = halves(first_ref[...], second_ref[...])
    next_k = exact(pair, exact(gram_k, pair), TN)
    next_m = exact(pair, exact(gram_m, pair), TN)
    firsto_ref[0:64] = jnp.concatenate([next_k[0:64, 0:64], next_m[0:64, 0:64]], 1)
    firsto_ref[64:128] = jnp.concatenate([next_k[64:128, 0:64], next_m[64:128, 0:64]], 1)
    firsto_ref[128:192] = jnp.concatenate([next_k[64:128, 64:128], next_m[64:128, 64:128]], 1)
    (inv,) = factor_inverses([sym(next_k[0:64, 0:64])])
    inv_ref[...] = inv


def second_search(
    total_rows, first_ref, second_ref, ready_ref, kv_ref, mv_ref, ks_ref, ms_ref, kd_ref, s_ref, pair_ref
):
    mixing, gram_k, _ = chain(first_ref[...], second_ref[...], ready_ref[...], total_rows)
    pair_ref[...] = both(mixing)
    ritz = sym(exact(mixing, exact(gram_k, mixing), TN)) * (1.0 / total_rows)
    weights = split(jnp.concatenate([mixing, -exact(mixing, ritz)], 0))
    for b in range(0, s_ref.shape[1], 512):
        at = slice(b, b + 512)
        parts = split(jnp.concatenate([kv_ref[:, at], ks_ref[:, at], mv_ref[:, at], ms_ref[:, at]], 0))
        s_ref[:, at] = dot3(weights, parts, TN) / kd_ref[:, at]


def mix(pair, xp_ref, s_ref, at):
    return dot3(pair, split(jnp.concatenate([xp_ref[:, at], s_ref[:, at]], 0)), TN)


def mix_pair(pair_ref, xp_ref, s_ref, xpo_ref):
    pair = split(pair_ref[...])
    for b in range(0, s_ref.shape[1], 512):
        at = slice(b, b + 512)
        xpo_ref[:, at] = mix(pair, xp_ref, s_ref, at)


def last_kernel(total_rows, first_ref, second_ref, ready_ref, xp_ref, s_ref, xo_ref, po_ref):
    mixing, _, _ = chain(first_ref[...], second_ref[...], ready_ref[...], total_rows)
    pair = split(both(mixing))
    for b in range(0, s_ref.shape[1], 512):
        at = slice(b, b + 512)
        new = mix(pair, xp_ref, s_ref, at)
        xo_ref[:, at] = new[0:64]
        po_ref[:, at] = new[64:128]


def whole():
    return pl.BlockSpec(memory_space=pltpu.VMEM)


def smem():
    return pl.BlockSpec(memory_space=pltpu.SMEM)


def anywhere():
    return pl.BlockSpec(memory_space=pl.ANY)


def f32(*shape):
    return jax.ShapeDtypeStruct(shape, jnp.float32)


def bf16_blocks(extended, rows):
    return [pltpu.VMEM((extended, rows, BS), jnp.bfloat16)] * 2


def call(kernel, name, ins, outs, shapes, scratch=(), grid=None, aliases=None, flops=0, moved=0):
    kwargs = {} if grid is None else {"grid": grid}
    return pl.pallas_call(
        kernel,
        in_specs=ins,
        out_specs=outs,
        out_shape=shapes,
        scratch_shapes=list(scratch),
        input_output_aliases=aliases or {},
        compiler_params=pltpu.CompilerParams(vmem_limit_bytes=VMEM_LIMIT),
        cost_estimate=pl.CostEstimate(flops=flops, bytes_accessed=moved, transcendentals=0),
        name=name,
        **kwargs,
    )


def shards(start_block, prior_direction, col_index, k_blocks, m_blocks, k_diagonal, m_diagonal):
    blocks = col_index.shape[0]
    rows = start_block.shape[1]
    devices = lax.axis_size("slab") * lax.axis_size("row")
    total_rows = float(rows * devices)
    edge = FACE * BS
    first_block = (lax.axis_index("slab") * lax.axis_size("row") + lax.axis_index("row")) * blocks - FACE
    col = col_index - first_block
    kd, md = k_diagonal[None, :], m_diagonal[None, :]
    inner, outer = ((blocks - 2 * FACE) // STEP,), (2,)
    last = blocks // STEP - 1
    extended = blocks + 2 * FACE

    def stored(at):
        blocked = pl.BlockSpec((STEP, NNZ, BS, BS), lambda i: (at(i), 0, 0, 0))
        return [blocked] * 2 + columns(1, at)

    def columns(height, at):
        return [pl.BlockSpec((height, STEP * BS), lambda i: (0, at(i)))] * 2

    def inside(i):
        return i + 1

    def at_edge(i):
        return i * last

    def edges(v):
        return v[:, :edge], v[:, rows - edge :]

    big = {"flops": 3 * 2 * 2 * 128 * 384 * 256 * blocks, "moved": 8 * blocks * NNZ * BS * BS}
    matrices = (k_blocks, m_blocks, kd, md)

    xp = jnp.concatenate([start_block, prior_direction], 0)
    low, high, _ = exchange(edges(xp))
    kv, mv, part = call(
        pair_inner, "pair_inner",
        [smem(), whole()] + stored(inside),
        columns(128, inside) + [whole()],
        [f32(128, rows), f32(128, rows), f32(256, 128)],
        bf16_blocks(extended, 128), inner, **big,
    )(col, xp, *matrices)
    kv, mv, gram = call(
        pair_edges, "pair_edges",
        [smem()] + [whole()] * 4 + [anywhere()] * 2 + stored(at_edge),
        columns(128, at_edge) + [whole()],
        [f32(128, rows), f32(128, rows), f32(192, 128)],
        bf16_blocks(extended, 128) + [pltpu.VMEM((256, 128), jnp.float32)], outer, {5: 0, 6: 1},
    )(col, xp, low, high, part, kv, mv, *matrices)

    first = all_sum(gram)

    s, inv = call(
        first_search, "first_search", [whole()] * 4, [whole()] * 2, [f32(64, rows), f32(64, 64)]
    )(first, kv, mv, kd)

    def factor(first, inv):
        return call(factor_pair, "factor_pair", [whole()] * 2, whole(), f32(320, 64))(first, inv)

    low, high, ready = exchange(edges(s), lambda: factor(first, inv))
    ks, ms, part = call(
        lambda *refs: search_inner(True, *refs), "search_inner",
        [smem()] + [whole()] * 2 + stored(inside),
        columns(64, inside) + [whole()],
        [f32(64, rows), f32(64, rows), f32(128, 192)],
        bf16_blocks(extended, 64), inner, **big,
    )(col, xp, s, *matrices)
    ks, ms, gram = call(
        lambda *refs: search_edges(True, *refs), "search_edges",
        [smem()] + [whole()] * 5 + [anywhere()] * 2 + stored(at_edge),
        columns(64, at_edge) + [whole()],
        [f32(64, rows), f32(64, rows), f32(192, 128)],
        bf16_blocks(extended, 64) + [pltpu.VMEM((128, 192), jnp.float32)], outer, {6: 0, 7: 1},
    )(col, xp, s, low, high, part, ks, ms, *matrices)

    second = all_sum(gram)

    new, pair = call(
        lambda *refs: second_search(total_rows, *refs), "second_search",
        [whole()] * 8, [whole()] * 2, [f32(64, rows), f32(192, 128)],
    )(first, second, ready, kv, mv, ks, ms, kd)

    def grams():
        return call(
            next_first, "next_first", [whole()] * 3, [whole()] * 2, [f32(192, 128), f32(64, 64)]
        )(first, second, pair)

    low, high, (first, inv) = exchange(edges(new), grams)
    xp = call(mix_pair, "mix_pair", [whole()] * 3, whole(), f32(128, rows))(pair, xp, s)
    (part,) = call(
        lambda *refs: search_inner(False, *refs), "second_inner",
        [smem()] + [whole()] * 2 + stored(inside), [whole()], [f32(128, 192)],
        bf16_blocks(extended, 64), inner, **big,
    )(col, xp, new, *matrices)
    (gram,) = call(
        lambda *refs: search_edges(False, *refs), "second_edges",
        [smem()] + [whole()] * 5 + stored(at_edge), [whole()], [f32(192, 128)],
        bf16_blocks(extended, 64) + [pltpu.VMEM((128, 192), jnp.float32)], outer,
    )(col, xp, new, low, high, part, *matrices)

    second, ready = all_sum(gram, (first, inv), [factor])

    iterate, prior = call(
        lambda *refs: last_kernel(total_rows, *refs), "last_mix",
        [whole()] * 5, [whole()] * 2, [f32(64, rows)] * 2,
    )(first, second, ready, xp, new)
    return (iterate, prior)


def solution(mesh):
    in_specs = (
        P(None, ("slab", "row")),
        P(None, ("slab", "row")),
        P(("slab", "row"), None),
        P(("slab", "row"), None, None, None),
        P(("slab", "row"), None, None, None),
        P(("slab", "row")),
        P(("slab", "row")),
    )
    out_specs = (P(None, ("slab", "row")), P(None, ("slab", "row")))
    return jax.shard_map(shards, mesh=mesh, in_specs=in_specs, out_specs=out_specs, check_vma=False)
```

```python
import jax
import jax.numpy as jnp
from jax import lax
from jax.experimental import pallas as pl
from jax.experimental.pallas import tpu as pltpu
from jax.sharding import PartitionSpec as P

COLS = 64
BS = 128
FACE = 2
NNZ = 3
AXES = ("slab", "row")
HIGHEST = lax.Precision.HIGHEST
STEP = 2
VMEM_LIMIT = 48 * 1024 * 1024


def coords(i):
    zh, c, y, x, zl = i & 1, (i >> 1) & 1, (i >> 2) & 3, (i >> 4) & 3, (i >> 6) & 3
    return {"x": x, "y": y, "z": zh * 4 + zl, "c": c}


def flat(d):
    zh, zl = d["z"] >> 2, d["z"] & 3
    return (((zl * 4 + d["x"]) * 4 + d["y"]) * 2 + d["c"]) * 2 + zh


def partner(x, axis, k):
    pairs = []
    for i in range(256):
        d = coords(i)
        d[axis] ^= k
        pairs.append((i, flat(d)))
    return lax.ppermute(x, AXES, pairs)


ROUNDS = (("c", (1,)), ("x", (1, 2, 3)), ("y", (1, 2, 3)), ("z", (1, 2, 3)), ("z", (4,)))


def all_sum(x, given=None, tasks=None):
    for n, (axis, ks) in enumerate(ROUNDS):
        task = (tasks or {}).get(n)
        if task is not None:
            x, given = lax.optimization_barrier((x, given))
            given = task(*given)
        for part in [partner(x, axis, k) for k in ks]:
            x = x + part
        if task is not None:
            x, given = lax.optimization_barrier((x, given))
    return (x, given) if tasks else x


def exchange(edges):
    head, tail = edges
    count = lax.axis_size("slab") * lax.axis_size("row")
    low = lax.ppermute(tail, AXES, [(i, i + 1) for i in range(count - 1)])
    return low, lax.ppermute(head, AXES, [(i + 1, i) for i in range(count - 1)])


def split(x):
    hi = x.astype(jnp.bfloat16)
    return hi, (x - hi.astype(jnp.float32)).astype(jnp.bfloat16)


def dot3(a, b, dims):
    def dot(u, v):
        return lax.dot_general(u, v, (dims, ((), ())), preferred_element_type=jnp.float32)

    return dot(a[0], b[0]) + (dot(a[0], b[1]) + dot(a[1], b[0]))


NT = ((1,), (1,))
TN = ((0,), (0,))
NN = ((1,), (0,))


def exact(a, b, dims=NN):
    return lax.dot_general(a, b, (dims, ((), ())), precision=HIGHEST, preferred_element_type=jnp.float32)


def sym(a):
    return 0.5 * (a + a.T)


def factor_inverses(mats):
    rows = lax.broadcasted_iota(jnp.int32, (COLS, 1), 0)
    eye = (
        lax.broadcasted_iota(jnp.int32, (COLS, COLS), 0) == lax.broadcasted_iota(jnp.int32, (COLS, COLS), 1)
    ).astype(jnp.float32)
    work = [jnp.concatenate([a, eye], 1) for a in mats]
    for j in range(0, COLS, 2):
        for n, w in enumerate(work):
            r1, r2 = w[j : j + 1, :], w[j + 1 : j + 2, :]
            a, b, c = r1[:, j : j + 1], r1[:, j + 1 : j + 2], r2[:, j + 1 : j + 2]
            scale = 1.0 / (a * c - b * b)
            u1, u2 = (c * r1 - b * r2) * scale, (a * r2 - b * r1) * scale
            below = w[:, j : j + 1] * u1 + w[:, j + 1 : j + 2] * u2
            work[n] = w - jnp.where(rows > j + 1, below, jnp.where(rows == j + 1, (b / a) * r1, 0.0))
    out = []
    for w in work:
        d = jnp.sum(w[:, :COLS] * eye, axis=1, keepdims=True)
        r = lax.rsqrt(d)
        r = r * (1.5 - 0.5 * d * r * r)
        out.append(w[:, COLS:] * r)
    return out


def first_parts(first):
    return (
        (sym(first[0:64, 0:64]), first[64:128, 0:64], sym(first[128:192, 0:64])),
        (sym(first[0:64, 64:128]), first[64:128, 64:128], sym(first[128:192, 64:128])),
    )


def halves(first, second):
    out = []
    for n, (xx, px, pp) in enumerate(first_parts(first)):
        sx, sp = second[64 * n : 64 * n + 64, 0:64], second[64 * n : 64 * n + 64, 64:128]
        ss = sym(second[128:192, 64 * n : 64 * n + 64])
        out.append(
            jnp.concatenate(
                [
                    jnp.concatenate([xx, px.T, sx.T], 1),
                    jnp.concatenate([px, pp, sp.T], 1),
                    jnp.concatenate([sx, sp, ss], 1),
                ],
                0,
            )
        )
    return out


def prepare(first, l1, out_ref):
    (_, px_k, pp_k), (xx_m, px_m, _) = first_parts(first)
    y1 = exact(l1, xx_m)
    l21 = exact(px_k, l1, NT)
    (l2,) = factor_inverses([pp_k - exact(l21, l21, NT)])
    y2 = exact(l2, px_m - exact(l21, y1))
    for n, part in enumerate((l1, l2, l21, y1, y2)):
        out_ref[64 * n : 64 * n + 64] = part


def chain(first, second, ready, total_rows):
    l1, l2, l21, y1, y2 = (ready[64 * n : 64 * n + 64] for n in range(5))
    gram_k, gram_m = halves(first, second)
    sx_k, sp_k, ss_k, sx_m = gram_k[128:, 0:64], gram_k[128:, 64:128], gram_k[128:, 128:], gram_m[128:, 0:64]
    l31 = exact(sx_k, l1, NT)
    l32 = exact(sp_k - exact(l31, l21, NT), l2, NT)
    (l3,) = factor_inverses([ss_k - exact(l31, l31, NT) - exact(l32, l32, NT)])
    z3 = exact(l3, exact(l3, sx_m - exact(l31, y1) - exact(l32, y2)), TN)
    z2 = exact(l2, y2 - exact(l32, z3, TN), TN)
    z1 = exact(l1, y1 - exact(l21, z2, TN) - exact(l31, z3, TN), TN)
    coeffs = jnp.concatenate([z1, z2, z3], 0)
    norm = sym(exact(coeffs, exact(gram_m, coeffs), TN))
    (ln,) = factor_inverses([norm * (1.0 / total_rows)])
    return exact(coeffs, ln, NT), gram_k, gram_m


def both(mixing):
    return jnp.concatenate([mixing, jnp.concatenate([jnp.zeros((64, 64), jnp.float32), mixing[64:]], 0)], 1)


def block_row(t, g, col_ref, k_ref, m_ref, hi_ref, lo_ref):
    acc = None
    for j in range(NNZ):
        at = col_ref[g, j]
        w = split(jnp.concatenate([k_ref[t, j], m_ref[t, j]], 0))
        term = dot3((hi_ref[at], lo_ref[at]), w, NT)
        acc = term if acc is None else acc + term
    return acc


def fill(hi_ref, lo_ref, at, tiles):
    for b in range(tiles.shape[1] // BS):
        hi_ref[at + b], lo_ref[at + b] = split(tiles[:, b * BS : (b + 1) * BS])


def pair_steps(first, col_ref, xp_ref, k_ref, m_ref, kd_ref, md_ref, kv_ref, mv_ref, hi_ref, lo_ref, acc_ref):
    for t in range(STEP):
        g = first + t
        at = slice(t * BS, (t + 1) * BS)
        acc = block_row(t, g, col_ref, k_ref, m_ref, hi_ref, lo_ref)
        tile = xp_ref[:, pl.ds(pl.multiple_of(g * BS, BS), BS)]
        kv = acc[:, :BS] + kd_ref[:, at] * tile
        mv = acc[:, BS:] + md_ref[:, at] * tile
        kv_ref[:, at] = kv
        mv_ref[:, at] = mv
        acc_ref[...] += dot3(split(jnp.concatenate([kv, mv], 0)), (hi_ref[g + FACE], lo_ref[g + FACE]), NT)


def pair_inner(col_ref, xp_ref, k_ref, m_ref, kd_ref, md_ref, kv_ref, mv_ref, acc_ref, hi_ref, lo_ref):
    i = pl.program_id(0)

    @pl.when(i == 0)
    def _():
        acc_ref[...] = jnp.zeros_like(acc_ref)
        fill(hi_ref, lo_ref, FACE, xp_ref[...])

    pair_steps(i * STEP + FACE, col_ref, xp_ref, k_ref, m_ref, kd_ref, md_ref, kv_ref, mv_ref, hi_ref, lo_ref, acc_ref)


def fill_edges(v_ref, low_ref, high_ref, hi_ref, lo_ref):
    rows = v_ref.shape[1]
    blocks = rows // BS
    fill(hi_ref, lo_ref, 0, low_ref[...])
    fill(hi_ref, lo_ref, FACE, v_ref[:, : 2 * FACE * BS])
    fill(hi_ref, lo_ref, blocks - FACE, v_ref[:, rows - 2 * FACE * BS :])
    fill(hi_ref, lo_ref, FACE + blocks, high_ref[...])
    return blocks


def pair_edges(
    col_ref, xp_ref, low_ref, high_ref, part_ref, kvin_ref, mvin_ref, k_ref, m_ref, kd_ref, md_ref,
    kv_ref, mv_ref, gram_ref, hi_ref, lo_ref, acc_ref,
):
    i = pl.program_id(0)

    @pl.when(i == 0)
    def _():
        acc_ref[...] = part_ref[...]
        fill_edges(xp_ref, low_ref, high_ref, hi_ref, lo_ref)

    first = i * (xp_ref.shape[1] // BS - FACE)
    pair_steps(first, col_ref, xp_ref, k_ref, m_ref, kd_ref, md_ref, kv_ref, mv_ref, hi_ref, lo_ref, acc_ref)

    @pl.when(i == pl.num_programs(0) - 1)
    def _():
        gram = acc_ref[...]
        gram_ref[0:64] = jnp.concatenate([gram[0:64, 0:64], gram[128:192, 0:64]], 1)
        gram_ref[64:128] = jnp.concatenate([gram[64:128, 0:64], gram[192:256, 0:64]], 1)
        gram_ref[128:192] = jnp.concatenate([gram[64:128, 64:128], gram[192:256, 64:128]], 1)


def first_search(first_ref, kv_ref, mv_ref, kd_ref, s_ref, inv_ref):
    (xx_k, _, _), (xx_m, _, _) = first_parts(first_ref[...])
    inv, inv_k = factor_inverses([xx_m, xx_k])
    inv_ref[...] = inv_k
    ritz = split(exact(inv, exact(inv, xx_k), TN))
    for b in range(0, s_ref.shape[1], 512):
        at = slice(b, b + 512)
        s_ref[:, at] = (kv_ref[0:64, at] - dot3(ritz, split(mv_ref[0:64, at]), TN)) / kd_ref[:, at]


def search_steps(first, col_ref, xp_ref, s_ref, k_ref, m_ref, kd_ref, md_ref, out, hi_ref, lo_ref, acc_ref):
    for t in range(STEP):
        g = first + t
        at = slice(t * BS, (t + 1) * BS)
        here = pl.ds(pl.multiple_of(g * BS, BS), BS)
        acc = block_row(t, g, col_ref, k_ref, m_ref, hi_ref, lo_ref)
        s = s_ref[:, here]
        ks = acc[:, :BS] + kd_ref[:, at] * s
        ms = acc[:, BS:] + md_ref[:, at] * s
        if out:
            out[0][:, at] = ks
            out[1][:, at] = ms
        basis = tuple(jnp.concatenate([u, v[g + FACE]], 0) for u, v in zip(split(xp_ref[:, here]), (hi_ref, lo_ref)))
        acc_ref[...] += dot3(split(jnp.concatenate([ks, ms], 0)), basis, NT)


def search_inner(col_ref, xp_ref, s_ref, k_ref, m_ref, kd_ref, md_ref, *rest):
    *out, acc_ref, hi_ref, lo_ref = rest
    i = pl.program_id(0)

    @pl.when(i == 0)
    def _():
        acc_ref[...] = jnp.zeros_like(acc_ref)
        fill(hi_ref, lo_ref, FACE, s_ref[...])

    search_steps(i * STEP + FACE, col_ref, xp_ref, s_ref, k_ref, m_ref, kd_ref, md_ref, out, hi_ref, lo_ref, acc_ref)


def search_edges(keep, col_ref, xp_ref, s_ref, low_ref, high_ref, part_ref, *rest):
    k_ref, m_ref, kd_ref, md_ref, *out, gram_ref, hi_ref, lo_ref, acc_ref = rest[2:] if keep else rest
    i = pl.program_id(0)

    @pl.when(i == 0)
    def _():
        acc_ref[...] = part_ref[...]
        fill_edges(s_ref, low_ref, high_ref, hi_ref, lo_ref)

    first = i * (s_ref.shape[1] // BS - FACE)
    search_steps(first, col_ref, xp_ref, s_ref, k_ref, m_ref, kd_ref, md_ref, out, hi_ref, lo_ref, acc_ref)

    @pl.when(i == pl.num_programs(0) - 1)
    def _():
        gram = acc_ref[...]
        gram_ref[0:128] = gram[:, 0:128]
        gram_ref[128:192] = jnp.concatenate([gram[0:64, 128:192], gram[64:128, 128:192]], 1)


def factor_pair(first_ref, inv_ref, ready_ref):
    prepare(first_ref[...], inv_ref[...], ready_ref)


def next_first(first_ref, second_ref, pair_ref, firsto_ref, inv_ref):
    pair = pair_ref[...]
    gram_k, gram_m = halves(first_ref[...], second_ref[...])
    next_k = exact(pair, exact(gram_k, pair), TN)
    next_m = exact(pair, exact(gram_m, pair), TN)
    firsto_ref[0:64] = jnp.concatenate([next_k[0:64, 0:64], next_m[0:64, 0:64]], 1)
    firsto_ref[64:128] = jnp.concatenate([next_k[64:128, 0:64], next_m[64:128, 0:64]], 1)
    firsto_ref[128:192] = jnp.concatenate([next_k[64:128, 64:128], next_m[64:128, 64:128]], 1)
    (inv,) = factor_inverses([sym(next_k[0:64, 0:64])])
    inv_ref[...] = inv


def second_search(
    total_rows, first_ref, second_ref, ready_ref, kv_ref, mv_ref, ks_ref, ms_ref, kd_ref, s_ref, pair_ref
):
    mixing, gram_k, _ = chain(first_ref[...], second_ref[...], ready_ref[...], total_rows)
    pair_ref[...] = both(mixing)
    ritz = sym(exact(mixing, exact(gram_k, mixing), TN)) * (1.0 / total_rows)
    weights = split(jnp.concatenate([mixing, -exact(mixing, ritz)], 0))
    for b in range(0, s_ref.shape[1], 512):
        at = slice(b, b + 512)
        parts = split(jnp.concatenate([kv_ref[:, at], ks_ref[:, at], mv_ref[:, at], ms_ref[:, at]], 0))
        s_ref[:, at] = dot3(weights, parts, TN) / kd_ref[:, at]


def mix(pair, xp_ref, s_ref, at):
    return dot3(pair, split(jnp.concatenate([xp_ref[:, at], s_ref[:, at]], 0)), TN)


def mix_pair(pair_ref, xp_ref, s_ref, xpo_ref):
    pair = split(pair_ref[...])
    for b in range(0, s_ref.shape[1], 512):
        at = slice(b, b + 512)
        xpo_ref[:, at] = mix(pair, xp_ref, s_ref, at)


def last_kernel(total_rows, first_ref, second_ref, ready_ref, xp_ref, s_ref, xo_ref, po_ref):
    mixing, _, _ = chain(first_ref[...], second_ref[...], ready_ref[...], total_rows)
    pair = split(both(mixing))
    for b in range(0, s_ref.shape[1], 512):
        at = slice(b, b + 512)
        new = mix(pair, xp_ref, s_ref, at)
        xo_ref[:, at] = new[0:64]
        po_ref[:, at] = new[64:128]


def whole():
    return pl.BlockSpec(memory_space=pltpu.VMEM)


def smem():
    return pl.BlockSpec(memory_space=pltpu.SMEM)


def anywhere():
    return pl.BlockSpec(memory_space=pl.ANY)


def f32(*shape):
    return jax.ShapeDtypeStruct(shape, jnp.float32)


def bf16_blocks(extended, rows):
    return [pltpu.VMEM((extended, rows, BS), jnp.bfloat16)] * 2


def call(kernel, name, ins, outs, shapes, scratch=(), grid=None, aliases=None, flops=0, moved=0):
    kwargs = {} if grid is None else {"grid": grid}
    return pl.pallas_call(
        kernel,
        in_specs=ins,
        out_specs=outs,
        out_shape=shapes,
        scratch_shapes=list(scratch),
        input_output_aliases=aliases or {},
        compiler_params=pltpu.CompilerParams(vmem_limit_bytes=VMEM_LIMIT),
        cost_estimate=pl.CostEstimate(flops=flops, bytes_accessed=moved, transcendentals=0),
        name=name,
        **kwargs,
    )


def shards(start_block, prior_direction, col_index, k_blocks, m_blocks, k_diagonal, m_diagonal):
    blocks = col_index.shape[0]
    rows = start_block.shape[1]
    devices = lax.axis_size("slab") * lax.axis_size("row")
    total_rows = float(rows * devices)
    edge = FACE * BS
    first_block = (lax.axis_index("slab") * lax.axis_size("row") + lax.axis_index("row")) * blocks - FACE
    col = col_index - first_block
    kd, md = k_diagonal[None, :], m_diagonal[None, :]
    inner, outer = ((blocks - 2 * FACE) // STEP,), (2,)
    last = blocks // STEP - 1
    extended = blocks + 2 * FACE

    def stored(at):
        blocked = pl.BlockSpec((STEP, NNZ, BS, BS), lambda i: (at(i), 0, 0, 0))
        return [blocked] * 2 + columns(1, at)

    def columns(height, at):
        return [pl.BlockSpec((height, STEP * BS), lambda i: (0, at(i)))] * 2

    def inside(i):
        return i + 1

    def at_edge(i):
        return i * last

    def edges(v):
        return v[:, :edge], v[:, rows - edge :]

    big = {"flops": 3 * 2 * 2 * 128 * 384 * 256 * blocks, "moved": 8 * blocks * NNZ * BS * BS}
    matrices = (k_blocks, m_blocks, kd, md)

    xp = jnp.concatenate([start_block, prior_direction], 0)
    low, high = exchange(edges(xp))
    kv, mv, part = call(
        pair_inner, "pair_inner",
        [smem(), whole()] + stored(inside),
        columns(128, inside) + [whole()],
        [f32(128, rows), f32(128, rows), f32(256, 128)],
        bf16_blocks(extended, 128), inner, **big,
    )(col, xp, *matrices)
    kv, mv, gram = call(
        pair_edges, "pair_edges",
        [smem()] + [whole()] * 4 + [anywhere()] * 2 + stored(at_edge),
        columns(128, at_edge) + [whole()],
        [f32(128, rows), f32(128, rows), f32(192, 128)],
        bf16_blocks(extended, 128) + [pltpu.VMEM((256, 128), jnp.float32)], outer, {5: 0, 6: 1},
    )(col, xp, low, high, part, kv, mv, *matrices)

    first = all_sum(gram)

    s, inv = call(
        first_search, "first_search", [whole()] * 4, [whole()] * 2, [f32(64, rows), f32(64, 64)]
    )(first, kv, mv, kd)

    low, high = exchange(edges(s))
    ks, ms, part = call(
        search_inner, "search_inner",
        [smem()] + [whole()] * 2 + stored(inside),
        columns(64, inside) + [whole()],
        [f32(64, rows), f32(64, rows), f32(128, 192)],
        bf16_blocks(extended, 64), inner, **big,
    )(col, xp, s, *matrices)
    ks, ms, gram = call(
        lambda *refs: search_edges(True, *refs), "search_edges",
        [smem()] + [whole()] * 5 + [anywhere()] * 2 + stored(at_edge),
        columns(64, at_edge) + [whole()],
        [f32(64, rows), f32(64, rows), f32(192, 128)],
        bf16_blocks(extended, 64) + [pltpu.VMEM((128, 192), jnp.float32)], outer, {6: 0, 7: 1},
    )(col, xp, s, low, high, part, ks, ms, *matrices)

    def factor(first, inv):
        return first, call(factor_pair, "factor_pair", [whole()] * 2, whole(), f32(320, 64))(first, inv)

    second, (first, ready) = all_sum(gram, (first, inv), {4: factor})

    new, pair = call(
        lambda *refs: second_search(total_rows, *refs), "second_search",
        [whole()] * 8, [whole()] * 2, [f32(64, rows), f32(192, 128)],
    )(first, second, ready, kv, mv, ks, ms, kd)

    def grams(first, second, pair):
        return call(
            next_first, "next_first", [whole()] * 3, [whole()] * 2, [f32(192, 128), f32(64, 64)]
        )(first, second, pair)

    low, high = exchange(edges(new))
    xp = call(mix_pair, "mix_pair", [whole()] * 3, whole(), f32(128, rows))(pair, xp, s)
    (part,) = call(
        search_inner, "second_inner",
        [smem()] + [whole()] * 2 + stored(inside), [whole()], [f32(128, 192)],
        bf16_blocks(extended, 64), inner, **big,
    )(col, xp, new, *matrices)
    (gram,) = call(
        lambda *refs: search_edges(False, *refs), "second_edges",
        [smem()] + [whole()] * 5 + stored(at_edge), [whole()], [f32(192, 128)],
        bf16_blocks(extended, 64) + [pltpu.VMEM((128, 192), jnp.float32)], outer,
    )(col, xp, new, low, high, part, *matrices)

    second, (first, ready) = all_sum(gram, (first, second, pair), {3: grams, 4: factor})

    iterate, prior = call(
        lambda *refs: last_kernel(total_rows, *refs), "last_mix",
        [whole()] * 5, [whole()] * 2, [f32(64, rows)] * 2,
    )(first, second, ready, xp, new)
    return (iterate, prior)


def solution(mesh):
    in_specs = (
        P(None, ("slab", "row")),
        P(None, ("slab", "row")),
        P(("slab", "row"), None),
        P(("slab", "row"), None, None, None),
        P(("slab", "row"), None, None, None),
        P(("slab", "row")),
        P(("slab", "row")),
    )
    out_specs = (P(None, ("slab", "row")), P(None, ("slab", "row")))
    return jax.shard_map(shards, mesh=mesh, in_specs=in_specs, out_specs=out_specs, check_vma=False)
```

```python
import jax
import jax.numpy as jnp
from jax import lax
from jax.experimental import pallas as pl
from jax.experimental.pallas import tpu as pltpu
from jax.sharding import PartitionSpec as P

COLS = 64
BS = 128
FACE = 2
NNZ = 3
AXES = ("slab", "row")
HIGHEST = lax.Precision.HIGHEST
STEP = 2
QUARTER = 160
VMEM_LIMIT = 48 * 1024 * 1024


def coords(i):
    zh, c, y, x, zl = i & 1, (i >> 1) & 1, (i >> 2) & 3, (i >> 4) & 3, (i >> 6) & 3
    return {"x": x, "y": y, "z": zh * 4 + zl, "c": c}


def flat(d):
    zh, zl = d["z"] >> 2, d["z"] & 3
    return (((zl * 4 + d["x"]) * 4 + d["y"]) * 2 + d["c"]) * 2 + zh


def partner(x, axis, k):
    pairs = []
    for i in range(256):
        d = coords(i)
        d[axis] ^= k
        pairs.append((i, flat(d)))
    return lax.ppermute(x, AXES, pairs)


ROUNDS = (("c", (1,)), ("x", (1, 2, 3)), ("y", (1, 2, 3)), ("z", (1, 2, 3)), ("z", (4,)))


def all_sum(x, given=None, tasks=None):
    for n, (axis, ks) in enumerate(ROUNDS):
        task = (tasks or {}).get(n)
        if task is not None:
            x, given = lax.optimization_barrier((x, given))
            given = task(*given)
        for part in [partner(x, axis, k) for k in ks]:
            x = x + part
        if task is not None:
            x, given = lax.optimization_barrier((x, given))
    return (x, given) if tasks else x


def x_coord():
    return (lax.axis_index("slab") >> 3) & 3


def all_sum_quarters(quarters):
    own = quarters[0]
    for part in [partner(quarters[k], "x", k) for k in (1, 2, 3)]:
        own = own + part
    for axis, ks in ROUNDS:
        if axis != "x":
            for part in [partner(own, axis, k) for k in ks]:
                own = own + part
    return [own] + [partner(own, "x", k) for k in (1, 2, 3)]


def exchange(edges):
    head, tail = edges
    count = lax.axis_size("slab") * lax.axis_size("row")
    low = lax.ppermute(tail, AXES, [(i, i + 1) for i in range(count - 1)])
    return low, lax.ppermute(head, AXES, [(i + 1, i) for i in range(count - 1)])


def split(x):
    hi = x.astype(jnp.bfloat16)
    return hi, (x - hi.astype(jnp.float32)).astype(jnp.bfloat16)


def dot3(a, b, dims):
    def dot(u, v):
        return lax.dot_general(u, v, (dims, ((), ())), preferred_element_type=jnp.float32)

    return dot(a[0], b[0]) + (dot(a[0], b[1]) + dot(a[1], b[0]))


NT = ((1,), (1,))
TN = ((0,), (0,))
NN = ((1,), (0,))


def exact(a, b, dims=NN):
    return lax.dot_general(a, b, (dims, ((), ())), precision=HIGHEST, preferred_element_type=jnp.float32)


def sym(a):
    return 0.5 * (a + a.T)


def factor_inverses(mats):
    rows = lax.broadcasted_iota(jnp.int32, (COLS, 1), 0)
    eye = (
        lax.broadcasted_iota(jnp.int32, (COLS, COLS), 0) == lax.broadcasted_iota(jnp.int32, (COLS, COLS), 1)
    ).astype(jnp.float32)
    work = [jnp.concatenate([a, eye], 1) for a in mats]
    for j in range(0, COLS, 2):
        for n, w in enumerate(work):
            r1, r2 = w[j : j + 1, :], w[j + 1 : j + 2, :]
            a, b, c = r1[:, j : j + 1], r1[:, j + 1 : j + 2], r2[:, j + 1 : j + 2]
            scale = 1.0 / (a * c - b * b)
            u1, u2 = (c * r1 - b * r2) * scale, (a * r2 - b * r1) * scale
            below = w[:, j : j + 1] * u1 + w[:, j + 1 : j + 2] * u2
            work[n] = w - jnp.where(rows > j + 1, below, jnp.where(rows == j + 1, (b / a) * r1, 0.0))
    out = []
    for w in work:
        d = jnp.sum(w[:, :COLS] * eye, axis=1, keepdims=True)
        r = lax.rsqrt(d)
        r = r * (1.5 - 0.5 * d * r * r)
        out.append(w[:, COLS:] * r)
    return out


def first_parts(first):
    return (
        (sym(first[0:64, 0:64]), first[64:128, 0:64], sym(first[128:192, 0:64])),
        (sym(first[0:64, 64:128]), first[64:128, 64:128], sym(first[128:192, 64:128])),
    )


def halves(first, second):
    out = []
    for n, (xx, px, pp) in enumerate(first_parts(first)):
        sx, sp = second[64 * n : 64 * n + 64, 0:64], second[64 * n : 64 * n + 64, 64:128]
        ss = sym(second[128:192, 64 * n : 64 * n + 64])
        out.append(
            jnp.concatenate(
                [
                    jnp.concatenate([xx, px.T, sx.T], 1),
                    jnp.concatenate([px, pp, sp.T], 1),
                    jnp.concatenate([sx, sp, ss], 1),
                ],
                0,
            )
        )
    return out


def prepare(first, l1, out_ref):
    (_, px_k, pp_k), (xx_m, px_m, _) = first_parts(first)
    y1 = exact(l1, xx_m)
    l21 = exact(px_k, l1, NT)
    (l2,) = factor_inverses([pp_k - exact(l21, l21, NT)])
    y2 = exact(l2, px_m - exact(l21, y1))
    for n, part in enumerate((l1, l2, l21, y1, y2)):
        out_ref[64 * n : 64 * n + 64] = part


def chain(first, second, ready, total_rows):
    l1, l2, l21, y1, y2 = (ready[64 * n : 64 * n + 64] for n in range(5))
    gram_k, gram_m = halves(first, second)
    sx_k, sp_k, ss_k, sx_m = gram_k[128:, 0:64], gram_k[128:, 64:128], gram_k[128:, 128:], gram_m[128:, 0:64]
    l31 = exact(sx_k, l1, NT)
    l32 = exact(sp_k - exact(l31, l21, NT), l2, NT)
    (l3,) = factor_inverses([ss_k - exact(l31, l31, NT) - exact(l32, l32, NT)])
    z3 = exact(l3, exact(l3, sx_m - exact(l31, y1) - exact(l32, y2)), TN)
    z2 = exact(l2, y2 - exact(l32, z3, TN), TN)
    z1 = exact(l1, y1 - exact(l21, z2, TN) - exact(l31, z3, TN), TN)
    coeffs = jnp.concatenate([z1, z2, z3], 0)
    norm = sym(exact(coeffs, exact(gram_m, coeffs), TN))
    (ln,) = factor_inverses([norm * (1.0 / total_rows)])
    return exact(coeffs, ln, NT), gram_k, gram_m


def both(mixing):
    return jnp.concatenate([mixing, jnp.concatenate([jnp.zeros((64, 64), jnp.float32), mixing[64:]], 0)], 1)


def block_row(t, g, col_ref, k_ref, m_ref, hi_ref, lo_ref):
    acc = None
    for j in range(NNZ):
        at = col_ref[g, j]
        w = split(jnp.concatenate([k_ref[t, j], m_ref[t, j]], 0))
        term = dot3((hi_ref[at], lo_ref[at]), w, NT)
        acc = term if acc is None else acc + term
    return acc


def fill(hi_ref, lo_ref, at, tiles):
    for b in range(tiles.shape[1] // BS):
        hi_ref[at + b], lo_ref[at + b] = split(tiles[:, b * BS : (b + 1) * BS])


def pair_steps(first, col_ref, xp_ref, k_ref, m_ref, kd_ref, md_ref, out, hi_ref, lo_ref, acc_ref):
    kv_ref, mv_ref, parts_ref = out
    for t in range(STEP):
        g = first + t
        at = slice(t * BS, (t + 1) * BS)
        acc = block_row(t, g, col_ref, k_ref, m_ref, hi_ref, lo_ref)
        tile = xp_ref[:, pl.ds(pl.multiple_of(g * BS, BS), BS)]
        kv = acc[:, :BS] + kd_ref[:, at] * tile
        mv = acc[:, BS:] + md_ref[:, at] * tile
        kv_ref[:, at] = kv
        mv_ref[:, at] = mv
        parts_ref[:, at] = jnp.concatenate([kv[0:64], mv[0:64]], 0) / kd_ref[:, at]
        acc_ref[...] += dot3(split(jnp.concatenate([kv, mv], 0)), (hi_ref[g + FACE], lo_ref[g + FACE]), NT)


def pair_inner(col_ref, xp_ref, k_ref, m_ref, kd_ref, md_ref, kv_ref, mv_ref, parts_ref, acc_ref, hi_ref, lo_ref):
    i = pl.program_id(0)

    @pl.when(i == 0)
    def _():
        acc_ref[...] = jnp.zeros_like(acc_ref)
        fill(hi_ref, lo_ref, FACE, xp_ref[...])

    out = (kv_ref, mv_ref, parts_ref)
    pair_steps(i * STEP + FACE, col_ref, xp_ref, k_ref, m_ref, kd_ref, md_ref, out, hi_ref, lo_ref, acc_ref)


def fill_edges(v_ref, low_ref, high_ref, hi_ref, lo_ref):
    rows = v_ref.shape[1]
    blocks = rows // BS
    fill(hi_ref, lo_ref, 0, low_ref[...])
    fill(hi_ref, lo_ref, FACE, v_ref[:, : 2 * FACE * BS])
    fill(hi_ref, lo_ref, blocks - FACE, v_ref[:, rows - 2 * FACE * BS :])
    fill(hi_ref, lo_ref, FACE + blocks, high_ref[...])
    return blocks


def pair_edges(
    col_ref, xp_ref, low_ref, high_ref, part_ref, kvin_ref, mvin_ref, partsin_ref, k_ref, m_ref, kd_ref, md_ref,
    kv_ref, mv_ref, parts_ref, gram_ref, hi_ref, lo_ref, acc_ref,
):
    i = pl.program_id(0)

    @pl.when(i == 0)
    def _():
        acc_ref[...] = part_ref[...]
        fill_edges(xp_ref, low_ref, high_ref, hi_ref, lo_ref)

    first = i * (xp_ref.shape[1] // BS - FACE)
    out = (kv_ref, mv_ref, parts_ref)
    pair_steps(first, col_ref, xp_ref, k_ref, m_ref, kd_ref, md_ref, out, hi_ref, lo_ref, acc_ref)

    @pl.when(i == pl.num_programs(0) - 1)
    def _():
        gram = acc_ref[...]
        gram_ref[0:64] = jnp.concatenate([gram[0:64, 0:64], gram[128:192, 0:64]], 1)
        gram_ref[64:128] = jnp.concatenate([gram[64:128, 0:64], gram[192:256, 0:64]], 1)
        gram_ref[128:192] = jnp.concatenate([gram[64:128, 64:128], gram[192:256, 64:128]], 1)


def parts_steps(first, col_ref, xp_ref, parts_ref, k_ref, m_ref, kd_ref, md_ref, kv_ref, mv_ref, hi_ref, lo_ref, acc_ref):
    for t in range(STEP):
        g = first + t
        at = slice(t * BS, (t + 1) * BS)
        here = pl.ds(pl.multiple_of(g * BS, BS), BS)
        acc = block_row(t, g, col_ref, k_ref, m_ref, hi_ref, lo_ref)
        tile = parts_ref[:, here]
        kv = acc[:, :BS] + kd_ref[:, at] * tile
        mv = acc[:, BS:] + md_ref[:, at] * tile
        kv_ref[:, at] = kv
        mv_ref[:, at] = mv
        basis = tuple(jnp.concatenate([u, v[g + FACE]], 0) for u, v in zip(split(xp_ref[:, here]), (hi_ref, lo_ref)))
        acc_ref[...] += dot3(split(jnp.concatenate([kv, mv], 0)), basis, NT)


def parts_inner(col_ref, xp_ref, parts_ref, k_ref, m_ref, kd_ref, md_ref, kv_ref, mv_ref, acc_ref, hi_ref, lo_ref):
    i = pl.program_id(0)

    @pl.when(i == 0)
    def _():
        acc_ref[...] = jnp.zeros_like(acc_ref)
        fill(hi_ref, lo_ref, FACE, parts_ref[...])

    parts_steps(
        i * STEP + FACE, col_ref, xp_ref, parts_ref, k_ref, m_ref, kd_ref, md_ref, kv_ref, mv_ref, hi_ref, lo_ref, acc_ref
    )


def parts_edges(
    col_ref, at_ref, xp_ref, parts_ref, low_ref, high_ref, part_ref, gram_ref, kvin_ref, mvin_ref, k_ref, m_ref, kd_ref, md_ref,
    kv_ref, mv_ref, q0_ref, q1_ref, q2_ref, q3_ref, hi_ref, lo_ref, acc_ref, all_ref,
):
    i = pl.program_id(0)

    @pl.when(i == 0)
    def _():
        acc_ref[...] = part_ref[...]
        fill_edges(parts_ref, low_ref, high_ref, hi_ref, lo_ref)

    first = i * (xp_ref.shape[1] // BS - FACE)
    parts_steps(
        first, col_ref, xp_ref, parts_ref, k_ref, m_ref, kd_ref, md_ref, kv_ref, mv_ref, hi_ref, lo_ref, acc_ref
    )

    @pl.when(i == pl.num_programs(0) - 1)
    def _():
        gram = acc_ref[...]
        all_ref[0:192] = gram_ref[...]
        all_ref[192:448] = gram[:, 0:128]
        all_ref[448:512] = jnp.concatenate([gram[0:64, 128:192], gram[128:192, 128:192]], 1)
        all_ref[512:576] = jnp.concatenate([gram[64:128, 128:192], gram[192:256, 128:192]], 1)
        all_ref[576:640] = jnp.concatenate([gram[64:128, 192:256], gram[192:256, 192:256]], 1)
        for k, out in enumerate((q0_ref, q1_ref, q2_ref, q3_ref)):
            out[...] = all_ref[pl.ds(pl.multiple_of((at_ref[0] ^ k) * QUARTER, 8), QUARTER), :]


def search_steps(first, col_ref, xp_ref, s_ref, k_ref, m_ref, kd_ref, md_ref, hi_ref, lo_ref, acc_ref):
    for t in range(STEP):
        g = first + t
        at = slice(t * BS, (t + 1) * BS)
        here = pl.ds(pl.multiple_of(g * BS, BS), BS)
        acc = block_row(t, g, col_ref, k_ref, m_ref, hi_ref, lo_ref)
        s = s_ref[:, here]
        ks = acc[:, :BS] + kd_ref[:, at] * s
        ms = acc[:, BS:] + md_ref[:, at] * s
        basis = tuple(jnp.concatenate([u, v[g + FACE]], 0) for u, v in zip(split(xp_ref[:, here]), (hi_ref, lo_ref)))
        acc_ref[...] += dot3(split(jnp.concatenate([ks, ms], 0)), basis, NT)


def search_inner(col_ref, xp_ref, s_ref, k_ref, m_ref, kd_ref, md_ref, acc_ref, hi_ref, lo_ref):
    i = pl.program_id(0)

    @pl.when(i == 0)
    def _():
        acc_ref[...] = jnp.zeros_like(acc_ref)
        fill(hi_ref, lo_ref, FACE, s_ref[...])

    search_steps(i * STEP + FACE, col_ref, xp_ref, s_ref, k_ref, m_ref, kd_ref, md_ref, hi_ref, lo_ref, acc_ref)


def search_edges(col_ref, xp_ref, s_ref, low_ref, high_ref, part_ref, k_ref, m_ref, kd_ref, md_ref, gram_ref, hi_ref, lo_ref, acc_ref):
    i = pl.program_id(0)

    @pl.when(i == 0)
    def _():
        acc_ref[...] = part_ref[...]
        fill_edges(s_ref, low_ref, high_ref, hi_ref, lo_ref)

    first = i * (s_ref.shape[1] // BS - FACE)
    search_steps(first, col_ref, xp_ref, s_ref, k_ref, m_ref, kd_ref, md_ref, hi_ref, lo_ref, acc_ref)

    @pl.when(i == pl.num_programs(0) - 1)
    def _():
        gram = acc_ref[...]
        gram_ref[0:128] = gram[:, 0:128]
        gram_ref[128:192] = jnp.concatenate([gram[0:64, 128:192], gram[64:128, 128:192]], 1)


def factor_pair(first_ref, inv_ref, ready_ref):
    prepare(first_ref[...], inv_ref[...], ready_ref)


def next_first(first_ref, second_ref, pair_ref, firsto_ref, inv_ref):
    pair = pair_ref[...]
    gram_k, gram_m = halves(first_ref[...], second_ref[...])
    next_k = exact(pair, exact(gram_k, pair), TN)
    next_m = exact(pair, exact(gram_m, pair), TN)
    firsto_ref[0:64] = jnp.concatenate([next_k[0:64, 0:64], next_m[0:64, 0:64]], 1)
    firsto_ref[64:128] = jnp.concatenate([next_k[64:128, 0:64], next_m[64:128, 0:64]], 1)
    firsto_ref[128:192] = jnp.concatenate([next_k[64:128, 64:128], next_m[64:128, 64:128]], 1)
    (inv,) = factor_inverses([sym(next_k[0:64, 0:64])])
    inv_ref[...] = inv


def search_gram(both_parts, ritz):
    one = jnp.concatenate([both_parts[192:256], both_parts[320:384]], 1)
    two = jnp.concatenate([both_parts[256:320], both_parts[384:448]], 1)
    crossed = jnp.concatenate([both_parts[512:576], both_parts[576:640]], 1)
    old = one - exact(ritz, two, TN)
    crossed = exact(ritz, crossed, TN)
    own = []
    for n in range(2):
        at = slice(64 * n, 64 * n + 64)
        mixed = crossed[:, at]
        own.append(sym(both_parts[448:512, at]) - mixed - mixed.T + exact(crossed[:, 128 + 64 * n : 192 + 64 * n], ritz))
    return jnp.concatenate([old[:, 0:128], old[:, 128:256], jnp.concatenate(own, 1)], 0)


def second_search(
    total_rows, at_ref, q0_ref, q1_ref, q2_ref, q3_ref, kv_ref, mv_ref, ks_ref, ms_ref, kd_ref,
    s_ref, pair_ref, spread_ref, first_ref, second_ref, all_ref, ready_ref,
):
    for k, quarter in enumerate((q0_ref, q1_ref, q2_ref, q3_ref)):
        all_ref[pl.ds(pl.multiple_of((at_ref[0] ^ k) * QUARTER, 8), QUARTER), :] = quarter[...]
    first = all_ref[0:192]
    first_ref[...] = first
    (xx_k, _, _), (xx_m, _, _) = first_parts(first)
    inv, inv_k = factor_inverses([xx_m, xx_k])
    ritz = exact(inv, exact(inv, xx_k), TN)
    prepare(first, inv_k, ready_ref)
    second = search_gram(all_ref[...], ritz)
    second_ref[...] = second
    mixing, gram_k, _ = chain(first, second, ready_ref[...], total_rows)
    pair = both(mixing)
    pair_ref[...] = pair
    spread = jnp.concatenate([pair, -exact(ritz, pair[128:192])], 0)
    spread_ref[...] = spread
    new_ritz = sym(exact(mixing, exact(gram_k, mixing), TN)) * (1.0 / total_rows)
    weights = split(jnp.concatenate([spread[:, 0:64], -exact(spread[:, 0:64], new_ritz)], 0))
    for b in range(0, s_ref.shape[1], 512):
        at = slice(b, b + 512)
        parts = split(jnp.concatenate([kv_ref[:, at], ks_ref[:, at], mv_ref[:, at], ms_ref[:, at]], 0))
        s_ref[:, at] = dot3(weights, parts, TN) / kd_ref[:, at]


def mix(pair, xp_ref, s_ref, at):
    return dot3(pair, split(jnp.concatenate([xp_ref[:, at], s_ref[:, at]], 0)), TN)


def mix_pair(pair_ref, xp_ref, s_ref, xpo_ref):
    pair = split(pair_ref[...])
    for b in range(0, s_ref.shape[1], 512):
        at = slice(b, b + 512)
        xpo_ref[:, at] = mix(pair, xp_ref, s_ref, at)


def last_kernel(total_rows, first_ref, second_ref, ready_ref, xp_ref, s_ref, xo_ref, po_ref):
    mixing, _, _ = chain(first_ref[...], second_ref[...], ready_ref[...], total_rows)
    pair = split(both(mixing))
    for b in range(0, s_ref.shape[1], 512):
        at = slice(b, b + 512)
        new = mix(pair, xp_ref, s_ref, at)
        xo_ref[:, at] = new[0:64]
        po_ref[:, at] = new[64:128]


def whole():
    return pl.BlockSpec(memory_space=pltpu.VMEM)


def smem():
    return pl.BlockSpec(memory_space=pltpu.SMEM)


def anywhere():
    return pl.BlockSpec(memory_space=pl.ANY)


def f32(*shape):
    return jax.ShapeDtypeStruct(shape, jnp.float32)


def bf16_blocks(extended, rows):
    return [pltpu.VMEM((extended, rows, BS), jnp.bfloat16)] * 2


def call(kernel, name, ins, outs, shapes, scratch=(), grid=None, aliases=None, flops=0, moved=0):
    kwargs = {} if grid is None else {"grid": grid}
    return pl.pallas_call(
        kernel,
        in_specs=ins,
        out_specs=outs,
        out_shape=shapes,
        scratch_shapes=list(scratch),
        input_output_aliases=aliases or {},
        compiler_params=pltpu.CompilerParams(vmem_limit_bytes=VMEM_LIMIT),
        cost_estimate=pl.CostEstimate(flops=flops, bytes_accessed=moved, transcendentals=0),
        name=name,
        **kwargs,
    )


def shards(start_block, prior_direction, col_index, k_blocks, m_blocks, k_diagonal, m_diagonal):
    blocks = col_index.shape[0]
    rows = start_block.shape[1]
    devices = lax.axis_size("slab") * lax.axis_size("row")
    total_rows = float(rows * devices)
    edge = FACE * BS
    first_block = (lax.axis_index("slab") * lax.axis_size("row") + lax.axis_index("row")) * blocks - FACE
    col = col_index - first_block
    kd, md = k_diagonal[None, :], m_diagonal[None, :]
    inner, outer = ((blocks - 2 * FACE) // STEP,), (2,)
    last = blocks // STEP - 1
    extended = blocks + 2 * FACE

    def stored(at):
        blocked = pl.BlockSpec((STEP, NNZ, BS, BS), lambda i: (at(i), 0, 0, 0))
        return [blocked] * 2 + columns(1, at)

    def columns(height, at, count=2):
        return [pl.BlockSpec((height, STEP * BS), lambda i: (0, at(i)))] * count

    def inside(i):
        return i + 1

    def at_edge(i):
        return i * last

    def edges(v):
        return v[:, :edge], v[:, rows - edge :]

    big = {"flops": 3 * 2 * 2 * 128 * 384 * 256 * blocks, "moved": 8 * blocks * NNZ * BS * BS}
    matrices = (k_blocks, m_blocks, kd, md)

    xp = jnp.concatenate([start_block, prior_direction], 0)
    low, high = exchange(edges(xp))
    kv, mv, parts, part = call(
        pair_inner, "pair_inner",
        [smem(), whole()] + stored(inside),
        columns(128, inside, 3) + [whole()],
        [f32(128, rows)] * 3 + [f32(256, 128)],
        bf16_blocks(extended, 128), inner, **big,
    )(col, xp, *matrices)
    kv, mv, parts, gram = call(
        pair_edges, "pair_edges",
        [smem()] + [whole()] * 4 + [anywhere()] * 3 + stored(at_edge),
        columns(128, at_edge, 3) + [whole()],
        [f32(128, rows)] * 3 + [f32(192, 128)],
        bf16_blocks(extended, 128) + [pltpu.VMEM((256, 128), jnp.float32)], outer, {5: 0, 6: 1, 7: 2},
    )(col, xp, low, high, part, kv, mv, parts, *matrices)

    low, high = exchange(edges(parts))
    ks, ms, part = call(
        parts_inner, "parts_inner",
        [smem()] + [whole()] * 2 + stored(inside),
        columns(128, inside) + [whole()],
        [f32(128, rows), f32(128, rows), f32(256, 256)],
        bf16_blocks(extended, 128), inner, **big,
    )(col, xp, parts, *matrices)
    at = x_coord().astype(jnp.int32)[None]
    ks, ms, *quarters = call(
        parts_edges, "parts_edges",
        [smem()] * 2 + [whole()] * 6 + [anywhere()] * 2 + stored(at_edge),
        columns(128, at_edge) + [whole()] * 4,
        [f32(128, rows), f32(128, rows)] + [f32(QUARTER, 128)] * 4,
        bf16_blocks(extended, 128) + [pltpu.VMEM((256, 256), jnp.float32), pltpu.VMEM((4 * QUARTER, 128), jnp.float32)],
        outer, {8: 0, 9: 1},
    )(col, at, xp, parts, low, high, part, gram, ks, ms, *matrices)

    quarters = all_sum_quarters(quarters)

    new, pair, spread, first, second = call(
        lambda *refs: second_search(total_rows, *refs), "second_search",
        [smem()] + [whole()] * 9, [whole()] * 5,
        [f32(64, rows), f32(192, 128), f32(256, 128), f32(192, 128), f32(192, 128)],
        [pltpu.VMEM((4 * QUARTER, 128), jnp.float32), pltpu.VMEM((320, 64), jnp.float32)],
    )(at, *quarters, kv, mv, ks, ms, kd)

    def factor(first, inv):
        return first, call(factor_pair, "factor_pair", [whole()] * 2, whole(), f32(320, 64))(first, inv)

    def grams(first, second, pair):
        return call(
            next_first, "next_first", [whole()] * 3, [whole()] * 2, [f32(192, 128), f32(64, 64)]
        )(first, second, pair)

    low, high = exchange(edges(new))
    xp = call(mix_pair, "mix_pair", [whole()] * 3, whole(), f32(128, rows))(spread, xp, parts)
    (part,) = call(
        search_inner, "second_inner",
        [smem()] + [whole()] * 2 + stored(inside), [whole()], [f32(128, 192)],
        bf16_blocks(extended, 64), inner, **big,
    )(col, xp, new, *matrices)
    (gram,) = call(
        search_edges, "second_edges",
        [smem()] + [whole()] * 5 + stored(at_edge), [whole()], [f32(192, 128)],
        bf16_blocks(extended, 64) + [pltpu.VMEM((128, 192), jnp.float32)], outer,
    )(col, xp, new, low, high, part, *matrices)

    second, (first, ready) = all_sum(gram, (first, second, pair), {3: grams, 4: factor})

    iterate, prior = call(
        lambda *refs: last_kernel(total_rows, *refs), "last_mix",
        [whole()] * 5, [whole()] * 2, [f32(64, rows)] * 2,
    )(first, second, ready, xp, new)
    return (iterate, prior)


def solution(mesh):
    in_specs = (
        P(None, ("slab", "row")),
        P(None, ("slab", "row")),
        P(("slab", "row"), None),
        P(("slab", "row"), None, None, None),
        P(("slab", "row"), None, None, None),
        P(("slab", "row")),
        P(("slab", "row")),
    )
    out_specs = (P(None, ("slab", "row")), P(None, ("slab", "row")))
    return jax.shard_map(shards, mesh=mesh, in_specs=in_specs, out_specs=out_specs, check_vma=False)
```

```python
import jax
import jax.numpy as jnp
from jax import lax
from jax.experimental import pallas as pl
from jax.experimental.pallas import tpu as pltpu
from jax.sharding import PartitionSpec as P

COLS = 64
BS = 128
FACE = 2
NNZ = 3
AXES = ("slab", "row")
HIGHEST = lax.Precision.HIGHEST
STEP = 2
PANEL = 8
QUARTER = 160
VMEM_LIMIT = 48 * 1024 * 1024


def coords(i):
    zh, c, y, x, zl = i & 1, (i >> 1) & 1, (i >> 2) & 3, (i >> 4) & 3, (i >> 6) & 3
    return {"x": x, "y": y, "z": zh * 4 + zl, "c": c}


def flat(d):
    zh, zl = d["z"] >> 2, d["z"] & 3
    return (((zl * 4 + d["x"]) * 4 + d["y"]) * 2 + d["c"]) * 2 + zh


def partner(x, axis, k):
    pairs = []
    for i in range(256):
        d = coords(i)
        d[axis] ^= k
        pairs.append((i, flat(d)))
    return lax.ppermute(x, AXES, pairs)


ROUNDS = (("c", (1,)), ("x", (1, 2, 3)), ("y", (1, 2, 3)), ("z", (1, 2, 3)), ("z", (4,)))


def all_sum(x, given=None, tasks=None):
    for n, (axis, ks) in enumerate(ROUNDS):
        task = (tasks or {}).get(n)
        if task is not None:
            x, given = lax.optimization_barrier((x, given))
            given = task(*given)
        for part in [partner(x, axis, k) for k in ks]:
            x = x + part
        if task is not None:
            x, given = lax.optimization_barrier((x, given))
    return (x, given) if tasks else x


def x_coord():
    return (lax.axis_index("slab") >> 3) & 3


def all_sum_quarters(quarters):
    own = quarters[0]
    for part in [partner(quarters[k], "x", k) for k in (1, 2, 3)]:
        own = own + part
    for axis, ks in ROUNDS:
        if axis != "x":
            for part in [partner(own, axis, k) for k in ks]:
                own = own + part
    return [own] + [partner(own, "x", k) for k in (1, 2, 3)]


def exchange(edges):
    head, tail = edges
    count = lax.axis_size("slab") * lax.axis_size("row")
    low = lax.ppermute(tail, AXES, [(i, i + 1) for i in range(count - 1)])
    return low, lax.ppermute(head, AXES, [(i + 1, i) for i in range(count - 1)])


def split(x):
    hi = x.astype(jnp.bfloat16)
    return hi, (x - hi.astype(jnp.float32)).astype(jnp.bfloat16)


def dot3(a, b, dims):
    def dot(u, v):
        return lax.dot_general(u, v, (dims, ((), ())), preferred_element_type=jnp.float32)

    return dot(a[0], b[0]) + (dot(a[0], b[1]) + dot(a[1], b[0]))


NT = ((1,), (1,))
TN = ((0,), (0,))
NN = ((1,), (0,))


def exact(a, b, dims=NN):
    return lax.dot_general(a, b, (dims, ((), ())), precision=HIGHEST, preferred_element_type=jnp.float32)


def sym(a):
    return 0.5 * (a + a.T)


def factor_inverses(mats):
    eye = (
        lax.broadcasted_iota(jnp.int32, (COLS, COLS), 0) == lax.broadcasted_iota(jnp.int32, (COLS, COLS), 1)
    ).astype(jnp.float32)
    work = [jnp.concatenate([a, eye], 1) for a in mats]
    done = [[] for _ in mats]
    for p in range(0, COLS, PANEL):
        left = COLS - p
        rows = lax.broadcasted_iota(jnp.int32, (left, 2 * COLS), 0)
        for n, w in enumerate(work):
            cols = [jnp.broadcast_to(w[:, p + k : p + k + 1], (left, 2 * COLS)) for k in range(PANEL)]
            for j in range(PANEL):
                factor = jnp.where(rows > j, cols[j] * (1.0 / cols[j][j : j + 1, :]), 0.0)
                for k in range(j + 1, PANEL):
                    cols[k] = cols[k] - factor * cols[k][j : j + 1, :]
                w = w - factor * w[j : j + 1, :]
            done[n].append(w[:PANEL])
            work[n] = w[PANEL:]
    out = []
    for parts in done:
        w = jnp.concatenate(parts, 0)
        d = jnp.sum(w[:, :COLS] * eye, axis=1, keepdims=True)
        r = lax.rsqrt(d)
        r = r * (1.5 - 0.5 * d * r * r)
        out.append(w[:, COLS:] * r)
    return out


def first_parts(first):
    return (
        (sym(first[0:64, 0:64]), first[64:128, 0:64], sym(first[128:192, 0:64])),
        (sym(first[0:64, 64:128]), first[64:128, 64:128], sym(first[128:192, 64:128])),
    )


def halves(first, second):
    out = []
    for n, (xx, px, pp) in enumerate(first_parts(first)):
        sx, sp = second[64 * n : 64 * n + 64, 0:64], second[64 * n : 64 * n + 64, 64:128]
        ss = sym(second[128:192, 64 * n : 64 * n + 64])
        out.append(
            jnp.concatenate(
                [
                    jnp.concatenate([xx, px.T, sx.T], 1),
                    jnp.concatenate([px, pp, sp.T], 1),
                    jnp.concatenate([sx, sp, ss], 1),
                ],
                0,
            )
        )
    return out


def prepare(first, l1, out_ref):
    (_, px_k, pp_k), (xx_m, px_m, _) = first_parts(first)
    y1 = exact(l1, xx_m)
    l21 = exact(px_k, l1, NT)
    (l2,) = factor_inverses([pp_k - exact(l21, l21, NT)])
    y2 = exact(l2, px_m - exact(l21, y1))
    for n, part in enumerate((l1, l2, l21, y1, y2)):
        out_ref[64 * n : 64 * n + 64] = part


def chain(first, second, ready, total_rows):
    l1, l2, l21, y1, y2 = (ready[64 * n : 64 * n + 64] for n in range(5))
    gram_k, gram_m = halves(first, second)
    sx_k, sp_k, ss_k, sx_m = gram_k[128:, 0:64], gram_k[128:, 64:128], gram_k[128:, 128:], gram_m[128:, 0:64]
    l31 = exact(sx_k, l1, NT)
    l32 = exact(sp_k - exact(l31, l21, NT), l2, NT)
    (l3,) = factor_inverses([ss_k - exact(l31, l31, NT) - exact(l32, l32, NT)])
    z3 = exact(l3, exact(l3, sx_m - exact(l31, y1) - exact(l32, y2)), TN)
    z2 = exact(l2, y2 - exact(l32, z3, TN), TN)
    z1 = exact(l1, y1 - exact(l21, z2, TN) - exact(l31, z3, TN), TN)
    coeffs = jnp.concatenate([z1, z2, z3], 0)
    norm = sym(exact(coeffs, exact(gram_m, coeffs), TN))
    (ln,) = factor_inverses([norm * (1.0 / total_rows)])
    return exact(coeffs, ln, NT), gram_k, gram_m


def both(mixing):
    return jnp.concatenate([mixing, jnp.concatenate([jnp.zeros((64, 64), jnp.float32), mixing[64:]], 0)], 1)


def block_row(t, g, col_ref, k_ref, m_ref, hi_ref, lo_ref):
    acc = None
    for j in range(NNZ):
        at = col_ref[g, j]
        w = split(jnp.concatenate([k_ref[t, j], m_ref[t, j]], 0))
        term = dot3((hi_ref[at], lo_ref[at]), w, NT)
        acc = term if acc is None else acc + term
    return acc


def fill(hi_ref, lo_ref, at, tiles):
    for b in range(tiles.shape[1] // BS):
        hi_ref[at + b], lo_ref[at + b] = split(tiles[:, b * BS : (b + 1) * BS])


def pair_steps(first, col_ref, xp_ref, k_ref, m_ref, kd_ref, md_ref, out, hi_ref, lo_ref, acc_ref):
    kv_ref, mv_ref, parts_ref = out
    for t in range(STEP):
        g = first + t
        at = slice(t * BS, (t + 1) * BS)
        acc = block_row(t, g, col_ref, k_ref, m_ref, hi_ref, lo_ref)
        tile = xp_ref[:, pl.ds(pl.multiple_of(g * BS, BS), BS)]
        kv = acc[:, :BS] + kd_ref[:, at] * tile
        mv = acc[:, BS:] + md_ref[:, at] * tile
        kv_ref[:, at] = kv
        mv_ref[:, at] = mv
        parts_ref[:, at] = jnp.concatenate([kv[0:64], mv[0:64]], 0) / kd_ref[:, at]
        acc_ref[...] += dot3(split(jnp.concatenate([kv, mv], 0)), (hi_ref[g + FACE], lo_ref[g + FACE]), NT)


def pair_inner(col_ref, xp_ref, k_ref, m_ref, kd_ref, md_ref, kv_ref, mv_ref, parts_ref, acc_ref, hi_ref, lo_ref):
    i = pl.program_id(0)

    @pl.when(i == 0)
    def _():
        acc_ref[...] = jnp.zeros_like(acc_ref)
        fill(hi_ref, lo_ref, FACE, xp_ref[...])

    out = (kv_ref, mv_ref, parts_ref)
    pair_steps(i * STEP + FACE, col_ref, xp_ref, k_ref, m_ref, kd_ref, md_ref, out, hi_ref, lo_ref, acc_ref)


def fill_edges(v_ref, low_ref, high_ref, hi_ref, lo_ref):
    rows = v_ref.shape[1]
    blocks = rows // BS
    fill(hi_ref, lo_ref, 0, low_ref[...])
    fill(hi_ref, lo_ref, FACE, v_ref[:, : 2 * FACE * BS])
    fill(hi_ref, lo_ref, blocks - FACE, v_ref[:, rows - 2 * FACE * BS :])
    fill(hi_ref, lo_ref, FACE + blocks, high_ref[...])
    return blocks


def pair_edges(
    col_ref, xp_ref, low_ref, high_ref, part_ref, kvin_ref, mvin_ref, partsin_ref, k_ref, m_ref, kd_ref, md_ref,
    kv_ref, mv_ref, parts_ref, gram_ref, hi_ref, lo_ref, acc_ref,
):
    i = pl.program_id(0)

    @pl.when(i == 0)
    def _():
        acc_ref[...] = part_ref[...]
        fill_edges(xp_ref, low_ref, high_ref, hi_ref, lo_ref)

    first = i * (xp_ref.shape[1] // BS - FACE)
    out = (kv_ref, mv_ref, parts_ref)
    pair_steps(first, col_ref, xp_ref, k_ref, m_ref, kd_ref, md_ref, out, hi_ref, lo_ref, acc_ref)

    @pl.when(i == pl.num_programs(0) - 1)
    def _():
        gram = acc_ref[...]
        gram_ref[0:64] = jnp.concatenate([gram[0:64, 0:64], gram[128:192, 0:64]], 1)
        gram_ref[64:128] = jnp.concatenate([gram[64:128, 0:64], gram[192:256, 0:64]], 1)
        gram_ref[128:192] = jnp.concatenate([gram[64:128, 64:128], gram[192:256, 64:128]], 1)


def parts_steps(first, col_ref, xp_ref, parts_ref, k_ref, m_ref, kd_ref, md_ref, kv_ref, mv_ref, hi_ref, lo_ref, acc_ref):
    for t in range(STEP):
        g = first + t
        at = slice(t * BS, (t + 1) * BS)
        here = pl.ds(pl.multiple_of(g * BS, BS), BS)
        acc = block_row(t, g, col_ref, k_ref, m_ref, hi_ref, lo_ref)
        tile = parts_ref[:, here]
        kv = acc[:, :BS] + kd_ref[:, at] * tile
        mv = acc[:, BS:] + md_ref[:, at] * tile
        kv_ref[:, at] = kv
        mv_ref[:, at] = mv
        basis = tuple(jnp.concatenate([u, v[g + FACE]], 0) for u, v in zip(split(xp_ref[:, here]), (hi_ref, lo_ref)))
        acc_ref[...] += dot3(split(jnp.concatenate([kv, mv], 0)), basis, NT)


def parts_inner(col_ref, xp_ref, parts_ref, k_ref, m_ref, kd_ref, md_ref, kv_ref, mv_ref, acc_ref, hi_ref, lo_ref):
    i = pl.program_id(0)

    @pl.when(i == 0)
    def _():
        acc_ref[...] = jnp.zeros_like(acc_ref)
        fill(hi_ref, lo_ref, FACE, parts_ref[...])

    parts_steps(
        i * STEP + FACE, col_ref, xp_ref, parts_ref, k_ref, m_ref, kd_ref, md_ref, kv_ref, mv_ref, hi_ref, lo_ref, acc_ref
    )


def parts_edges(
    col_ref, at_ref, xp_ref, parts_ref, low_ref, high_ref, part_ref, gram_ref, kvin_ref, mvin_ref, k_ref, m_ref, kd_ref, md_ref,
    kv_ref, mv_ref, q0_ref, q1_ref, q2_ref, q3_ref, hi_ref, lo_ref, acc_ref, all_ref,
):
    i = pl.program_id(0)

    @pl.when(i == 0)
    def _():
        acc_ref[...] = part_ref[...]
        fill_edges(parts_ref, low_ref, high_ref, hi_ref, lo_ref)

    first = i * (xp_ref.shape[1] // BS - FACE)
    parts_steps(
        first, col_ref, xp_ref, parts_ref, k_ref, m_ref, kd_ref, md_ref, kv_ref, mv_ref, hi_ref, lo_ref, acc_ref
    )

    @pl.when(i == pl.num_programs(0) - 1)
    def _():
        gram = acc_ref[...]
        all_ref[0:192] = gram_ref[...]
        all_ref[192:448] = gram[:, 0:128]
        all_ref[448:512] = jnp.concatenate([gram[0:64, 128:192], gram[128:192, 128:192]], 1)
        all_ref[512:576] = jnp.concatenate([gram[64:128, 128:192], gram[192:256, 128:192]], 1)
        all_ref[576:640] = jnp.concatenate([gram[64:128, 192:256], gram[192:256, 192:256]], 1)
        for k, out in enumerate((q0_ref, q1_ref, q2_ref, q3_ref)):
            out[...] = all_ref[pl.ds(pl.multiple_of((at_ref[0] ^ k) * QUARTER, 8), QUARTER), :]


def search_steps(first, col_ref, xp_ref, s_ref, k_ref, m_ref, kd_ref, md_ref, hi_ref, lo_ref, acc_ref):
    for t in range(STEP):
        g = first + t
        at = slice(t * BS, (t + 1) * BS)
        here = pl.ds(pl.multiple_of(g * BS, BS), BS)
        acc = block_row(t, g, col_ref, k_ref, m_ref, hi_ref, lo_ref)
        s = s_ref[:, here]
        ks = acc[:, :BS] + kd_ref[:, at] * s
        ms = acc[:, BS:] + md_ref[:, at] * s
        basis = tuple(jnp.concatenate([u, v[g + FACE]], 0) for u, v in zip(split(xp_ref[:, here]), (hi_ref, lo_ref)))
        acc_ref[...] += dot3(split(jnp.concatenate([ks, ms], 0)), basis, NT)


def search_inner(col_ref, xp_ref, s_ref, k_ref, m_ref, kd_ref, md_ref, acc_ref, hi_ref, lo_ref):
    i = pl.program_id(0)

    @pl.when(i == 0)
    def _():
        acc_ref[...] = jnp.zeros_like(acc_ref)
        fill(hi_ref, lo_ref, FACE, s_ref[...])

    search_steps(i * STEP + FACE, col_ref, xp_ref, s_ref, k_ref, m_ref, kd_ref, md_ref, hi_ref, lo_ref, acc_ref)


def search_edges(col_ref, xp_ref, s_ref, low_ref, high_ref, part_ref, k_ref, m_ref, kd_ref, md_ref, gram_ref, hi_ref, lo_ref, acc_ref):
    i = pl.program_id(0)

    @pl.when(i == 0)
    def _():
        acc_ref[...] = part_ref[...]
        fill_edges(s_ref, low_ref, high_ref, hi_ref, lo_ref)

    first = i * (s_ref.shape[1] // BS - FACE)
    search_steps(first, col_ref, xp_ref, s_ref, k_ref, m_ref, kd_ref, md_ref, hi_ref, lo_ref, acc_ref)

    @pl.when(i == pl.num_programs(0) - 1)
    def _():
        gram = acc_ref[...]
        gram_ref[0:128] = gram[:, 0:128]
        gram_ref[128:192] = jnp.concatenate([gram[0:64, 128:192], gram[64:128, 128:192]], 1)


def factor_pair(first_ref, inv_ref, ready_ref):
    prepare(first_ref[...], inv_ref[...], ready_ref)


def next_first(first_ref, second_ref, pair_ref, firsto_ref, inv_ref):
    pair = pair_ref[...]
    gram_k, gram_m = halves(first_ref[...], second_ref[...])
    next_k = exact(pair, exact(gram_k, pair), TN)
    next_m = exact(pair, exact(gram_m, pair), TN)
    firsto_ref[0:64] = jnp.concatenate([next_k[0:64, 0:64], next_m[0:64, 0:64]], 1)
    firsto_ref[64:128] = jnp.concatenate([next_k[64:128, 0:64], next_m[64:128, 0:64]], 1)
    firsto_ref[128:192] = jnp.concatenate([next_k[64:128, 64:128], next_m[64:128, 64:128]], 1)
    (inv,) = factor_inverses([sym(next_k[0:64, 0:64])])
    inv_ref[...] = inv


def search_gram(both_parts, ritz):
    one = jnp.concatenate([both_parts[192:256], both_parts[320:384]], 1)
    two = jnp.concatenate([both_parts[256:320], both_parts[384:448]], 1)
    crossed = jnp.concatenate([both_parts[512:576], both_parts[576:640]], 1)
    old = one - exact(ritz, two, TN)
    crossed = exact(ritz, crossed, TN)
    own = []
    for n in range(2):
        at = slice(64 * n, 64 * n + 64)
        mixed = crossed[:, at]
        own.append(sym(both_parts[448:512, at]) - mixed - mixed.T + exact(crossed[:, 128 + 64 * n : 192 + 64 * n], ritz))
    return jnp.concatenate([old[:, 0:128], old[:, 128:256], jnp.concatenate(own, 1)], 0)


def second_search(
    total_rows, at_ref, q0_ref, q1_ref, q2_ref, q3_ref, kv_ref, mv_ref, ks_ref, ms_ref, kd_ref,
    s_ref, pair_ref, spread_ref, first_ref, second_ref, all_ref, ready_ref,
):
    for k, quarter in enumerate((q0_ref, q1_ref, q2_ref, q3_ref)):
        all_ref[pl.ds(pl.multiple_of((at_ref[0] ^ k) * QUARTER, 8), QUARTER), :] = quarter[...]
    first = all_ref[0:192]
    first_ref[...] = first
    (xx_k, _, _), (xx_m, _, _) = first_parts(first)
    inv, inv_k = factor_inverses([xx_m, xx_k])
    ritz = exact(inv, exact(inv, xx_k), TN)
    prepare(first, inv_k, ready_ref)
    second = search_gram(all_ref[...], ritz)
    second_ref[...] = second
    mixing, gram_k, _ = chain(first, second, ready_ref[...], total_rows)
    pair = both(mixing)
    pair_ref[...] = pair
    spread = jnp.concatenate([pair, -exact(ritz, pair[128:192])], 0)
    spread_ref[...] = spread
    new_ritz = sym(exact(mixing, exact(gram_k, mixing), TN)) * (1.0 / total_rows)
    weights = split(jnp.concatenate([spread[:, 0:64], -exact(spread[:, 0:64], new_ritz)], 0))
    for b in range(0, s_ref.shape[1], 512):
        at = slice(b, b + 512)
        parts = split(jnp.concatenate([kv_ref[:, at], ks_ref[:, at], mv_ref[:, at], ms_ref[:, at]], 0))
        s_ref[:, at] = dot3(weights, parts, TN) / kd_ref[:, at]


def mix(pair, xp_ref, s_ref, at):
    return dot3(pair, split(jnp.concatenate([xp_ref[:, at], s_ref[:, at]], 0)), TN)


def mix_pair(pair_ref, xp_ref, s_ref, xpo_ref):
    pair = split(pair_ref[...])
    for b in range(0, s_ref.shape[1], 512):
        at = slice(b, b + 512)
        xpo_ref[:, at] = mix(pair, xp_ref, s_ref, at)


def last_kernel(total_rows, first_ref, second_ref, ready_ref, xp_ref, s_ref, xo_ref, po_ref):
    mixing, _, _ = chain(first_ref[...], second_ref[...], ready_ref[...], total_rows)
    pair = split(both(mixing))
    for b in range(0, s_ref.shape[1], 512):
        at = slice(b, b + 512)
        new = mix(pair, xp_ref, s_ref, at)
        xo_ref[:, at] = new[0:64]
        po_ref[:, at] = new[64:128]


def whole():
    return pl.BlockSpec(memory_space=pltpu.VMEM)


def smem():
    return pl.BlockSpec(memory_space=pltpu.SMEM)


def anywhere():
    return pl.BlockSpec(memory_space=pl.ANY)


def f32(*shape):
    return jax.ShapeDtypeStruct(shape, jnp.float32)


def bf16_blocks(extended, rows):
    return [pltpu.VMEM((extended, rows, BS), jnp.bfloat16)] * 2


def call(kernel, name, ins, outs, shapes, scratch=(), grid=None, aliases=None, flops=0, moved=0):
    kwargs = {} if grid is None else {"grid": grid}
    return pl.pallas_call(
        kernel,
        in_specs=ins,
        out_specs=outs,
        out_shape=shapes,
        scratch_shapes=list(scratch),
        input_output_aliases=aliases or {},
        compiler_params=pltpu.CompilerParams(vmem_limit_bytes=VMEM_LIMIT),
        cost_estimate=pl.CostEstimate(flops=flops, bytes_accessed=moved, transcendentals=0),
        name=name,
        **kwargs,
    )


def shards(start_block, prior_direction, col_index, k_blocks, m_blocks, k_diagonal, m_diagonal):
    blocks = col_index.shape[0]
    rows = start_block.shape[1]
    devices = lax.axis_size("slab") * lax.axis_size("row")
    total_rows = float(rows * devices)
    edge = FACE * BS
    first_block = (lax.axis_index("slab") * lax.axis_size("row") + lax.axis_index("row")) * blocks - FACE
    col = col_index - first_block
    kd, md = k_diagonal[None, :], m_diagonal[None, :]
    inner, outer = ((blocks - 2 * FACE) // STEP,), (2,)
    last = blocks // STEP - 1
    extended = blocks + 2 * FACE

    def stored(at):
        blocked = pl.BlockSpec((STEP, NNZ, BS, BS), lambda i: (at(i), 0, 0, 0))
        return [blocked] * 2 + columns(1, at)

    def columns(height, at, count=2):
        return [pl.BlockSpec((height, STEP * BS), lambda i: (0, at(i)))] * count

    def inside(i):
        return i + 1

    def at_edge(i):
        return i * last

    def edges(v):
        return v[:, :edge], v[:, rows - edge :]

    big = {"flops": 3 * 2 * 2 * 128 * 384 * 256 * blocks, "moved": 8 * blocks * NNZ * BS * BS}
    matrices = (k_blocks, m_blocks, kd, md)

    xp = jnp.concatenate([start_block, prior_direction], 0)
    low, high = exchange(edges(xp))
    kv, mv, parts, part = call(
        pair_inner, "pair_inner",
        [smem(), whole()] + stored(inside),
        columns(128, inside, 3) + [whole()],
        [f32(128, rows)] * 3 + [f32(256, 128)],
        bf16_blocks(extended, 128), inner, **big,
    )(col, xp, *matrices)
    kv, mv, parts, gram = call(
        pair_edges, "pair_edges",
        [smem()] + [whole()] * 4 + [anywhere()] * 3 + stored(at_edge),
        columns(128, at_edge, 3) + [whole()],
        [f32(128, rows)] * 3 + [f32(192, 128)],
        bf16_blocks(extended, 128) + [pltpu.VMEM((256, 128), jnp.float32)], outer, {5: 0, 6: 1, 7: 2},
    )(col, xp, low, high, part, kv, mv, parts, *matrices)

    low, high = exchange(edges(parts))
    ks, ms, part = call(
        parts_inner, "parts_inner",
        [smem()] + [whole()] * 2 + stored(inside),
        columns(128, inside) + [whole()],
        [f32(128, rows), f32(128, rows), f32(256, 256)],
        bf16_blocks(extended, 128), inner, **big,
    )(col, xp, parts, *matrices)
    at = x_coord().astype(jnp.int32)[None]
    ks, ms, *quarters = call(
        parts_edges, "parts_edges",
        [smem()] * 2 + [whole()] * 6 + [anywhere()] * 2 + stored(at_edge),
        columns(128, at_edge) + [whole()] * 4,
        [f32(128, rows), f32(128, rows)] + [f32(QUARTER, 128)] * 4,
        bf16_blocks(extended, 128) + [pltpu.VMEM((256, 256), jnp.float32), pltpu.VMEM((4 * QUARTER, 128), jnp.float32)],
        outer, {8: 0, 9: 1},
    )(col, at, xp, parts, low, high, part, gram, ks, ms, *matrices)

    quarters = all_sum_quarters(quarters)

    new, pair, spread, first, second = call(
        lambda *refs: second_search(total_rows, *refs), "second_search",
        [smem()] + [whole()] * 9, [whole()] * 5,
        [f32(64, rows), f32(192, 128), f32(256, 128), f32(192, 128), f32(192, 128)],
        [pltpu.VMEM((4 * QUARTER, 128), jnp.float32), pltpu.VMEM((320, 64), jnp.float32)],
    )(at, *quarters, kv, mv, ks, ms, kd)

    def factor(first, inv):
        return first, call(factor_pair, "factor_pair", [whole()] * 2, whole(), f32(320, 64))(first, inv)

    def grams(first, second, pair):
        return call(
            next_first, "next_first", [whole()] * 3, [whole()] * 2, [f32(192, 128), f32(64, 64)]
        )(first, second, pair)

    low, high = exchange(edges(new))
    xp = call(mix_pair, "mix_pair", [whole()] * 3, whole(), f32(128, rows))(spread, xp, parts)
    (part,) = call(
        search_inner, "second_inner",
        [smem()] + [whole()] * 2 + stored(inside), [whole()], [f32(128, 192)],
        bf16_blocks(extended, 64), inner, **big,
    )(col, xp, new, *matrices)
    (gram,) = call(
        search_edges, "second_edges",
        [smem()] + [whole()] * 5 + stored(at_edge), [whole()], [f32(192, 128)],
        bf16_blocks(extended, 64) + [pltpu.VMEM((128, 192), jnp.float32)], outer,
    )(col, xp, new, low, high, part, *matrices)

    second, (first, ready) = all_sum(gram, (first, second, pair), {3: grams, 4: factor})

    iterate, prior = call(
        lambda *refs: last_kernel(total_rows, *refs), "last_mix",
        [whole()] * 5, [whole()] * 2, [f32(64, rows)] * 2,
    )(first, second, ready, xp, new)
    return (iterate, prior)


def solution(mesh):
    in_specs = (
        P(None, ("slab", "row")),
        P(None, ("slab", "row")),
        P(("slab", "row"), None),
        P(("slab", "row"), None, None, None),
        P(("slab", "row"), None, None, None),
        P(("slab", "row")),
        P(("slab", "row")),
    )
    out_specs = (P(None, ("slab", "row")), P(None, ("slab", "row")))
    return jax.shard_map(shards, mesh=mesh, in_specs=in_specs, out_specs=out_specs, check_vma=False)
```

```python
import jax
import jax.numpy as jnp
from jax import lax
from jax.experimental import pallas as pl
from jax.experimental.pallas import tpu as pltpu
from jax.sharding import PartitionSpec as P

COLS = 64
BS = 128
FACE = 2
NNZ = 3
AXES = ("slab", "row")
HIGHEST = lax.Precision.HIGHEST
STEP = 2
PANEL = 8
QUARTER = 160
VMEM_LIMIT = 48 * 1024 * 1024


def coords(i):
    zh, c, y, x, zl = i & 1, (i >> 1) & 1, (i >> 2) & 3, (i >> 4) & 3, (i >> 6) & 3
    return {"x": x, "y": y, "z": zh * 4 + zl, "c": c}


def flat(d):
    zh, zl = d["z"] >> 2, d["z"] & 3
    return (((zl * 4 + d["x"]) * 4 + d["y"]) * 2 + d["c"]) * 2 + zh


def partner(x, axis, k):
    pairs = []
    for i in range(256):
        d = coords(i)
        d[axis] ^= k
        pairs.append((i, flat(d)))
    return lax.ppermute(x, AXES, pairs)


ROUNDS = (("c", (1,)), ("x", (1, 2, 3)), ("y", (1, 2, 3)), ("z", (1, 2, 3)), ("z", (4,)))


def all_sum(x, given=None, tasks=None):
    for n, (axis, ks) in enumerate(ROUNDS):
        task = (tasks or {}).get(n)
        if task is not None:
            x, given = lax.optimization_barrier((x, given))
            given = task(*given)
        for part in [partner(x, axis, k) for k in ks]:
            x = x + part
        if task is not None:
            x, given = lax.optimization_barrier((x, given))
    return (x, given) if tasks else x


def x_coord():
    return (lax.axis_index("slab") >> 3) & 3


def all_sum_quarters(quarters):
    own = quarters[0]
    for part in [partner(quarters[k], "x", k) for k in (1, 2, 3)]:
        own = own + part
    for axis, ks in ROUNDS:
        if axis != "x":
            for part in [partner(own, axis, k) for k in ks]:
                own = own + part
    return [own] + [partner(own, "x", k) for k in (1, 2, 3)]


def exchange(edges):
    head, tail = edges
    even = lax.axis_index("row") == 0
    count = lax.axis_size("slab") * lax.axis_size("row")
    near = [(i, i ^ 1) for i in range(count)]
    far = [(i, ((i + 1) ^ 1) - 1) for i in range(1, count - 1)]
    return (
        lax.ppermute(jnp.where(even, tail, head), AXES, near),
        lax.ppermute(jnp.where(even, head, tail), AXES, far),
    )


def split(x):
    hi = x.astype(jnp.bfloat16)
    return hi, (x - hi.astype(jnp.float32)).astype(jnp.bfloat16)


def dot3(a, b, dims):
    def dot(u, v):
        return lax.dot_general(u, v, (dims, ((), ())), preferred_element_type=jnp.float32)

    kept = 1 - dims[0][0]
    size = a[0].shape[kept]
    stacked = dot(jnp.concatenate(a, kept), b[0])
    return stacked[:size] + (dot(a[0], b[1]) + stacked[size:])


NT = ((1,), (1,))
TN = ((0,), (0,))
NN = ((1,), (0,))


def exact(a, b, dims=NN):
    return lax.dot_general(a, b, (dims, ((), ())), precision=HIGHEST, preferred_element_type=jnp.float32)


def sym(a):
    return 0.5 * (a + a.T)


def factor_inverses(mats):
    eye = (
        lax.broadcasted_iota(jnp.int32, (COLS, COLS), 0) == lax.broadcasted_iota(jnp.int32, (COLS, COLS), 1)
    ).astype(jnp.float32)
    work = [jnp.concatenate([a, eye], 1) for a in mats]
    done = [[] for _ in mats]
    for p in range(0, COLS, PANEL):
        left = COLS - p
        rows = lax.broadcasted_iota(jnp.int32, (left, 2 * COLS), 0)
        for n, w in enumerate(work):
            cols = [jnp.broadcast_to(w[:, p + k : p + k + 1], (left, 2 * COLS)) for k in range(PANEL)]
            for j in range(PANEL):
                factor = jnp.where(rows > j, cols[j] * (1.0 / cols[j][j : j + 1, :]), 0.0)
                for k in range(j + 1, PANEL):
                    cols[k] = cols[k] - factor * cols[k][j : j + 1, :]
                w = w - factor * w[j : j + 1, :]
            done[n].append(w[:PANEL])
            work[n] = w[PANEL:]
    out = []
    for parts in done:
        w = jnp.concatenate(parts, 0)
        d = jnp.sum(w[:, :COLS] * eye, axis=1, keepdims=True)
        r = lax.rsqrt(d)
        r = r * (1.5 - 0.5 * d * r * r)
        out.append(w[:, COLS:] * r)
    return out


def first_parts(first):
    return (
        (sym(first[0:64, 0:64]), first[64:128, 0:64], sym(first[128:192, 0:64])),
        (sym(first[0:64, 64:128]), first[64:128, 64:128], sym(first[128:192, 64:128])),
    )


def halves(first, second):
    out = []
    for n, (xx, px, pp) in enumerate(first_parts(first)):
        sx, sp = second[64 * n : 64 * n + 64, 0:64], second[64 * n : 64 * n + 64, 64:128]
        ss = sym(second[128:192, 64 * n : 64 * n + 64])
        out.append(
            jnp.concatenate(
                [
                    jnp.concatenate([xx, px.T, sx.T], 1),
                    jnp.concatenate([px, pp, sp.T], 1),
                    jnp.concatenate([sx, sp, ss], 1),
                ],
                0,
            )
        )
    return out


def prepare(first, l1, out_ref):
    (_, px_k, pp_k), (xx_m, px_m, _) = first_parts(first)
    y1 = exact(l1, xx_m)
    l21 = exact(px_k, l1, NT)
    (l2,) = factor_inverses([pp_k - exact(l21, l21, NT)])
    y2 = exact(l2, px_m - exact(l21, y1))
    for n, part in enumerate((l1, l2, l21, y1, y2)):
        out_ref[64 * n : 64 * n + 64] = part


def chain(first, second, ready, total_rows):
    l1, l2, l21, y1, y2 = (ready[64 * n : 64 * n + 64] for n in range(5))
    gram_k, gram_m = halves(first, second)
    sx_k, sp_k, ss_k, sx_m = gram_k[128:, 0:64], gram_k[128:, 64:128], gram_k[128:, 128:], gram_m[128:, 0:64]
    l31 = exact(sx_k, l1, NT)
    l32 = exact(sp_k - exact(l31, l21, NT), l2, NT)
    (l3,) = factor_inverses([ss_k - exact(l31, l31, NT) - exact(l32, l32, NT)])
    z3 = exact(l3, exact(l3, sx_m - exact(l31, y1) - exact(l32, y2)), TN)
    z2 = exact(l2, y2 - exact(l32, z3, TN), TN)
    z1 = exact(l1, y1 - exact(l21, z2, TN) - exact(l31, z3, TN), TN)
    coeffs = jnp.concatenate([z1, z2, z3], 0)
    norm = sym(exact(coeffs, exact(gram_m, coeffs), TN))
    (ln,) = factor_inverses([norm * (1.0 / total_rows)])
    return exact(coeffs, ln, NT), gram_k, gram_m


def both(mixing):
    return jnp.concatenate([mixing, jnp.concatenate([jnp.zeros((64, 64), jnp.float32), mixing[64:]], 0)], 1)


def block_row(t, g, col_ref, k_ref, m_ref, hi_ref, lo_ref):
    acc = None
    for j in range(NNZ):
        at = col_ref[g, j]
        w = split(jnp.concatenate([k_ref[t, j], m_ref[t, j]], 0))
        term = dot3((hi_ref[at], lo_ref[at]), w, NT)
        acc = term if acc is None else acc + term
    return acc


def fill(hi_ref, lo_ref, at, tiles):
    for b in range(tiles.shape[1] // BS):
        hi_ref[at + b], lo_ref[at + b] = split(tiles[:, b * BS : (b + 1) * BS])


def pair_steps(first, col_ref, xp_ref, k_ref, m_ref, kd_ref, md_ref, out, hi_ref, lo_ref, acc_ref):
    kv_ref, mv_ref, parts_ref = out
    for t in range(STEP):
        g = first + t
        at = slice(t * BS, (t + 1) * BS)
        acc = block_row(t, g, col_ref, k_ref, m_ref, hi_ref, lo_ref)
        tile = xp_ref[:, pl.ds(pl.multiple_of(g * BS, BS), BS)]
        kv = acc[:, :BS] + kd_ref[:, at] * tile
        mv = acc[:, BS:] + md_ref[:, at] * tile
        kv_ref[:, at] = kv
        mv_ref[:, at] = mv
        parts_ref[:, at] = jnp.concatenate([kv[0:64], mv[0:64]], 0) / kd_ref[:, at]
        acc_ref[...] += dot3(split(jnp.concatenate([kv, mv], 0)), (hi_ref[g + FACE], lo_ref[g + FACE]), NT)


def pair_inner(col_ref, xp_ref, k_ref, m_ref, kd_ref, md_ref, kv_ref, mv_ref, parts_ref, acc_ref, hi_ref, lo_ref):
    i = pl.program_id(0)

    @pl.when(i == 0)
    def _():
        acc_ref[...] = jnp.zeros_like(acc_ref)
        fill(hi_ref, lo_ref, FACE, xp_ref[...])

    out = (kv_ref, mv_ref, parts_ref)
    pair_steps(i * STEP + FACE, col_ref, xp_ref, k_ref, m_ref, kd_ref, md_ref, out, hi_ref, lo_ref, acc_ref)


def fill_edges(v_ref, at_ref, near_ref, far_ref, hi_ref, lo_ref):
    rows = v_ref.shape[1]
    blocks = rows // BS
    fill(hi_ref, lo_ref, (1 - at_ref[1]) * (FACE + blocks), near_ref[...])
    fill(hi_ref, lo_ref, at_ref[1] * (FACE + blocks), far_ref[...])
    fill(hi_ref, lo_ref, FACE, v_ref[:, : 2 * FACE * BS])
    fill(hi_ref, lo_ref, blocks - FACE, v_ref[:, rows - 2 * FACE * BS :])


def pair_edges(
    col_ref, at_ref, xp_ref, near_ref, far_ref, part_ref, kvin_ref, mvin_ref, partsin_ref, k_ref, m_ref, kd_ref, md_ref,
    kv_ref, mv_ref, parts_ref, gram_ref, hi_ref, lo_ref, acc_ref,
):
    i = pl.program_id(0)

    @pl.when(i == 0)
    def _():
        acc_ref[...] = part_ref[...]
        fill_edges(xp_ref, at_ref, near_ref, far_ref, hi_ref, lo_ref)

    first = i * (xp_ref.shape[1] // BS - FACE)
    out = (kv_ref, mv_ref, parts_ref)
    pair_steps(first, col_ref, xp_ref, k_ref, m_ref, kd_ref, md_ref, out, hi_ref, lo_ref, acc_ref)

    @pl.when(i == pl.num_programs(0) - 1)
    def _():
        gram = acc_ref[...]
        gram_ref[0:64] = jnp.concatenate([gram[0:64, 0:64], gram[128:192, 0:64]], 1)
        gram_ref[64:128] = jnp.concatenate([gram[64:128, 0:64], gram[192:256, 0:64]], 1)
        gram_ref[128:192] = jnp.concatenate([gram[64:128, 64:128], gram[192:256, 64:128]], 1)


def parts_steps(first, col_ref, xp_ref, parts_ref, k_ref, m_ref, kd_ref, md_ref, kv_ref, mv_ref, hi_ref, lo_ref, acc_ref):
    for t in range(STEP):
        g = first + t
        at = slice(t * BS, (t + 1) * BS)
        here = pl.ds(pl.multiple_of(g * BS, BS), BS)
        acc = block_row(t, g, col_ref, k_ref, m_ref, hi_ref, lo_ref)
        tile = parts_ref[:, here]
        kv = acc[:, :BS] + kd_ref[:, at] * tile
        mv = acc[:, BS:] + md_ref[:, at] * tile
        kv_ref[:, at] = kv
        mv_ref[:, at] = mv
        basis = tuple(jnp.concatenate([u, v[g + FACE]], 0) for u, v in zip(split(xp_ref[:, here]), (hi_ref, lo_ref)))
        acc_ref[...] += dot3(split(jnp.concatenate([kv, mv], 0)), basis, NT)


def parts_inner(col_ref, xp_ref, parts_ref, k_ref, m_ref, kd_ref, md_ref, kv_ref, mv_ref, acc_ref, hi_ref, lo_ref):
    i = pl.program_id(0)

    @pl.when(i == 0)
    def _():
        acc_ref[...] = jnp.zeros_like(acc_ref)
        fill(hi_ref, lo_ref, FACE, parts_ref[...])

    parts_steps(
        i * STEP + FACE, col_ref, xp_ref, parts_ref, k_ref, m_ref, kd_ref, md_ref, kv_ref, mv_ref, hi_ref, lo_ref, acc_ref
    )


def parts_edges(
    col_ref, at_ref, xp_ref, parts_ref, near_ref, far_ref, part_ref, gram_ref, kvin_ref, mvin_ref, k_ref, m_ref, kd_ref, md_ref,
    kv_ref, mv_ref, q0_ref, q1_ref, q2_ref, q3_ref, hi_ref, lo_ref, acc_ref, all_ref,
):
    i = pl.program_id(0)

    @pl.when(i == 0)
    def _():
        acc_ref[...] = part_ref[...]
        fill_edges(parts_ref, at_ref, near_ref, far_ref, hi_ref, lo_ref)

    first = i * (xp_ref.shape[1] // BS - FACE)
    parts_steps(
        first, col_ref, xp_ref, parts_ref, k_ref, m_ref, kd_ref, md_ref, kv_ref, mv_ref, hi_ref, lo_ref, acc_ref
    )

    @pl.when(i == pl.num_programs(0) - 1)
    def _():
        gram = acc_ref[...]
        all_ref[0:192] = gram_ref[...]
        all_ref[192:448] = gram[:, 0:128]
        all_ref[448:512] = jnp.concatenate([gram[0:64, 128:192], gram[128:192, 128:192]], 1)
        all_ref[512:576] = jnp.concatenate([gram[64:128, 128:192], gram[192:256, 128:192]], 1)
        all_ref[576:640] = jnp.concatenate([gram[64:128, 192:256], gram[192:256, 192:256]], 1)
        for k, out in enumerate((q0_ref, q1_ref, q2_ref, q3_ref)):
            out[...] = all_ref[pl.ds(pl.multiple_of((at_ref[0] ^ k) * QUARTER, 8), QUARTER), :]


def search_steps(first, col_ref, xp_ref, s_ref, k_ref, m_ref, kd_ref, md_ref, hi_ref, lo_ref, acc_ref):
    for t in range(STEP):
        g = first + t
        at = slice(t * BS, (t + 1) * BS)
        here = pl.ds(pl.multiple_of(g * BS, BS), BS)
        acc = block_row(t, g, col_ref, k_ref, m_ref, hi_ref, lo_ref)
        s = s_ref[:, here]
        ks = acc[:, :BS] + kd_ref[:, at] * s
        ms = acc[:, BS:] + md_ref[:, at] * s
        basis = tuple(jnp.concatenate([u, v[g + FACE]], 0) for u, v in zip(split(xp_ref[:, here]), (hi_ref, lo_ref)))
        acc_ref[...] += dot3(split(jnp.concatenate([ks, ms], 0)), basis, NT)


def search_inner(col_ref, xp_ref, s_ref, k_ref, m_ref, kd_ref, md_ref, acc_ref, hi_ref, lo_ref):
    i = pl.program_id(0)

    @pl.when(i == 0)
    def _():
        acc_ref[...] = jnp.zeros_like(acc_ref)
        fill(hi_ref, lo_ref, FACE, s_ref[...])

    search_steps(i * STEP + FACE, col_ref, xp_ref, s_ref, k_ref, m_ref, kd_ref, md_ref, hi_ref, lo_ref, acc_ref)


def search_edges(col_ref, at_ref, xp_ref, s_ref, near_ref, far_ref, part_ref, k_ref, m_ref, kd_ref, md_ref, gram_ref, hi_ref, lo_ref, acc_ref):
    i = pl.program_id(0)

    @pl.when(i == 0)
    def _():
        acc_ref[...] = part_ref[...]
        fill_edges(s_ref, at_ref, near_ref, far_ref, hi_ref, lo_ref)

    first = i * (s_ref.shape[1] // BS - FACE)
    search_steps(first, col_ref, xp_ref, s_ref, k_ref, m_ref, kd_ref, md_ref, hi_ref, lo_ref, acc_ref)

    @pl.when(i == pl.num_programs(0) - 1)
    def _():
        gram = acc_ref[...]
        gram_ref[0:128] = gram[:, 0:128]
        gram_ref[128:192] = jnp.concatenate([gram[0:64, 128:192], gram[64:128, 128:192]], 1)


def factor_pair(first_ref, inv_ref, ready_ref):
    prepare(first_ref[...], inv_ref[...], ready_ref)


def next_first(first_ref, second_ref, pair_ref, firsto_ref, inv_ref):
    pair = pair_ref[...]
    gram_k, gram_m = halves(first_ref[...], second_ref[...])
    next_k = exact(pair, exact(gram_k, pair), TN)
    next_m = exact(pair, exact(gram_m, pair), TN)
    firsto_ref[0:64] = jnp.concatenate([next_k[0:64, 0:64], next_m[0:64, 0:64]], 1)
    firsto_ref[64:128] = jnp.concatenate([next_k[64:128, 0:64], next_m[64:128, 0:64]], 1)
    firsto_ref[128:192] = jnp.concatenate([next_k[64:128, 64:128], next_m[64:128, 64:128]], 1)
    (inv,) = factor_inverses([sym(next_k[0:64, 0:64])])
    inv_ref[...] = inv


def search_gram(both_parts, ritz):
    one = jnp.concatenate([both_parts[192:256], both_parts[320:384]], 1)
    two = jnp.concatenate([both_parts[256:320], both_parts[384:448]], 1)
    crossed = jnp.concatenate([both_parts[512:576], both_parts[576:640]], 1)
    old = one - exact(ritz, two, TN)
    crossed = exact(ritz, crossed, TN)
    own = []
    for n in range(2):
        at = slice(64 * n, 64 * n + 64)
        mixed = crossed[:, at]
        own.append(sym(both_parts[448:512, at]) - mixed - mixed.T + exact(crossed[:, 128 + 64 * n : 192 + 64 * n], ritz))
    return jnp.concatenate([old[:, 0:128], old[:, 128:256], jnp.concatenate(own, 1)], 0)


def second_search(
    total_rows, at_ref, q0_ref, q1_ref, q2_ref, q3_ref, kv_ref, mv_ref, ks_ref, ms_ref, kd_ref,
    s_ref, pair_ref, spread_ref, first_ref, second_ref, all_ref, ready_ref,
):
    for k, quarter in enumerate((q0_ref, q1_ref, q2_ref, q3_ref)):
        all_ref[pl.ds(pl.multiple_of((at_ref[0] ^ k) * QUARTER, 8), QUARTER), :] = quarter[...]
    first = all_ref[0:192]
    first_ref[...] = first
    (xx_k, _, _), (xx_m, _, _) = first_parts(first)
    inv, inv_k = factor_inverses([xx_m, xx_k])
    ritz = exact(inv, exact(inv, xx_k), TN)
    prepare(first, inv_k, ready_ref)
    second = search_gram(all_ref[...], ritz)
    second_ref[...] = second
    mixing, gram_k, _ = chain(first, second, ready_ref[...], total_rows)
    pair = both(mixing)
    pair_ref[...] = pair
    spread = jnp.concatenate([pair, -exact(ritz, pair[128:192])], 0)
    spread_ref[...] = spread
    new_ritz = sym(exact(mixing, exact(gram_k, mixing), TN)) * (1.0 / total_rows)
    weights = split(jnp.concatenate([spread[:, 0:64], -exact(spread[:, 0:64], new_ritz)], 0))
    for b in range(0, s_ref.shape[1], 512):
        at = slice(b, b + 512)
        parts = split(jnp.concatenate([kv_ref[:, at], ks_ref[:, at], mv_ref[:, at], ms_ref[:, at]], 0))
        s_ref[:, at] = dot3(weights, parts, TN) / kd_ref[:, at]


def mix(pair, xp_ref, s_ref, at):
    return dot3(pair, split(jnp.concatenate([xp_ref[:, at], s_ref[:, at]], 0)), TN)


def mix_pair(pair_ref, xp_ref, s_ref, xpo_ref):
    pair = split(pair_ref[...])
    for b in range(0, s_ref.shape[1], 512):
        at = slice(b, b + 512)
        xpo_ref[:, at] = mix(pair, xp_ref, s_ref, at)


def last_kernel(total_rows, first_ref, second_ref, ready_ref, xp_ref, s_ref, xo_ref, po_ref):
    mixing, _, _ = chain(first_ref[...], second_ref[...], ready_ref[...], total_rows)
    pair = split(both(mixing))
    for b in range(0, s_ref.shape[1], 512):
        at = slice(b, b + 512)
        new = mix(pair, xp_ref, s_ref, at)
        xo_ref[:, at] = new[0:64]
        po_ref[:, at] = new[64:128]


def whole():
    return pl.BlockSpec(memory_space=pltpu.VMEM)


def smem():
    return pl.BlockSpec(memory_space=pltpu.SMEM)


def anywhere():
    return pl.BlockSpec(memory_space=pl.ANY)


def f32(*shape):
    return jax.ShapeDtypeStruct(shape, jnp.float32)


def bf16_blocks(extended, rows):
    return [pltpu.VMEM((extended, rows, BS), jnp.bfloat16)] * 2


def call(kernel, name, ins, outs, shapes, scratch=(), grid=None, aliases=None, flops=0, moved=0):
    kwargs = {} if grid is None else {"grid": grid}
    return pl.pallas_call(
        kernel,
        in_specs=ins,
        out_specs=outs,
        out_shape=shapes,
        scratch_shapes=list(scratch),
        input_output_aliases=aliases or {},
        compiler_params=pltpu.CompilerParams(vmem_limit_bytes=VMEM_LIMIT),
        cost_estimate=pl.CostEstimate(flops=flops, bytes_accessed=moved, transcendentals=0),
        name=name,
        **kwargs,
    )


def shards(start_block, prior_direction, col_index, k_blocks, m_blocks, k_diagonal, m_diagonal):
    blocks = col_index.shape[0]
    rows = start_block.shape[1]
    devices = lax.axis_size("slab") * lax.axis_size("row")
    total_rows = float(rows * devices)
    edge = FACE * BS
    first_block = (lax.axis_index("slab") * lax.axis_size("row") + lax.axis_index("row")) * blocks - FACE
    col = col_index - first_block
    kd, md = k_diagonal[None, :], m_diagonal[None, :]
    inner, outer = ((blocks - 2 * FACE) // STEP,), (2,)
    last = blocks // STEP - 1
    extended = blocks + 2 * FACE

    def stored(at):
        blocked = pl.BlockSpec((STEP, NNZ, BS, BS), lambda i: (at(i), 0, 0, 0))
        return [blocked] * 2 + columns(1, at)

    def columns(height, at, count=2):
        return [pl.BlockSpec((height, STEP * BS), lambda i: (0, at(i)))] * count

    def inside(i):
        return i + 1

    def at_edge(i):
        return i * last

    def edges(v):
        return v[:, :edge], v[:, rows - edge :]

    big = {"flops": 3 * 2 * 2 * 128 * 384 * 256 * blocks, "moved": 8 * blocks * NNZ * BS * BS}
    matrices = (k_blocks, m_blocks, kd, md)

    at = jnp.stack([x_coord(), lax.axis_index("row")]).astype(jnp.int32)
    xp = jnp.concatenate([start_block, prior_direction], 0)
    near, far = exchange(edges(xp))
    kv, mv, parts, part = call(
        pair_inner, "pair_inner",
        [smem(), whole()] + stored(inside),
        columns(128, inside, 3) + [whole()],
        [f32(128, rows)] * 3 + [f32(256, 128)],
        bf16_blocks(extended, 128), inner, **big,
    )(col, xp, *matrices)
    kv, mv, parts, gram = call(
        pair_edges, "pair_edges",
        [smem()] * 2 + [whole()] * 4 + [anywhere()] * 3 + stored(at_edge),
        columns(128, at_edge, 3) + [whole()],
        [f32(128, rows)] * 3 + [f32(192, 128)],
        bf16_blocks(extended, 128) + [pltpu.VMEM((256, 128), jnp.float32)], outer, {6: 0, 7: 1, 8: 2},
    )(col, at, xp, near, far, part, kv, mv, parts, *matrices)

    near, far = exchange(edges(parts))
    ks, ms, part = call(
        parts_inner, "parts_inner",
        [smem()] + [whole()] * 2 + stored(inside),
        columns(128, inside) + [whole()],
        [f32(128, rows), f32(128, rows), f32(256, 256)],
        bf16_blocks(extended, 128), inner, **big,
    )(col, xp, parts, *matrices)
    ks, ms, *quarters = call(
        parts_edges, "parts_edges",
        [smem()] * 2 + [whole()] * 6 + [anywhere()] * 2 + stored(at_edge),
        columns(128, at_edge) + [whole()] * 4,
        [f32(128, rows), f32(128, rows)] + [f32(QUARTER, 128)] * 4,
        bf16_blocks(extended, 128) + [pltpu.VMEM((256, 256), jnp.float32), pltpu.VMEM((4 * QUARTER, 128), jnp.float32)],
        outer, {8: 0, 9: 1},
    )(col, at, xp, parts, near, far, part, gram, ks, ms, *matrices)

    quarters = all_sum_quarters(quarters)

    new, pair, spread, first, second = call(
        lambda *refs: second_search(total_rows, *refs), "second_search",
        [smem()] + [whole()] * 9, [whole()] * 5,
        [f32(64, rows), f32(192, 128), f32(256, 128), f32(192, 128), f32(192, 128)],
        [pltpu.VMEM((4 * QUARTER, 128), jnp.float32), pltpu.VMEM((320, 64), jnp.float32)],
    )(at, *quarters, kv, mv, ks, ms, kd)

    def factor(first, inv):
        return first, call(factor_pair, "factor_pair", [whole()] * 2, whole(), f32(320, 64))(first, inv)

    def grams(first, second, pair):
        return call(
            next_first, "next_first", [whole()] * 3, [whole()] * 2, [f32(192, 128), f32(64, 64)]
        )(first, second, pair)

    near, far = exchange(edges(new))
    xp = call(mix_pair, "mix_pair", [whole()] * 3, whole(), f32(128, rows))(spread, xp, parts)
    (part,) = call(
        search_inner, "second_inner",
        [smem()] + [whole()] * 2 + stored(inside), [whole()], [f32(128, 192)],
        bf16_blocks(extended, 64), inner, **big,
    )(col, xp, new, *matrices)
    (gram,) = call(
        search_edges, "second_edges",
        [smem()] * 2 + [whole()] * 5 + stored(at_edge), [whole()], [f32(192, 128)],
        bf16_blocks(extended, 64) + [pltpu.VMEM((128, 192), jnp.float32)], outer,
    )(col, at, xp, new, near, far, part, *matrices)

    second, (first, ready) = all_sum(gram, (first, second, pair), {3: grams, 4: factor})

    iterate, prior = call(
        lambda *refs: last_kernel(total_rows, *refs), "last_mix",
        [whole()] * 5, [whole()] * 2, [f32(64, rows)] * 2,
    )(first, second, ready, xp, new)
    return (iterate, prior)


def solution(mesh):
    in_specs = (
        P(None, ("slab", "row")),
        P(None, ("slab", "row")),
        P(("slab", "row"), None),
        P(("slab", "row"), None, None, None),
        P(("slab", "row"), None, None, None),
        P(("slab", "row")),
        P(("slab", "row")),
    )
    out_specs = (P(None, ("slab", "row")), P(None, ("slab", "row")))
    return jax.shard_map(shards, mesh=mesh, in_specs=in_specs, out_specs=out_specs, check_vma=False)
```

```python
import jax
import jax.numpy as jnp
from jax import lax
from jax.experimental import pallas as pl
from jax.experimental.pallas import tpu as pltpu
from jax.sharding import PartitionSpec as P

COLS = 64
BS = 128
FACE = 2
NNZ = 3
AXES = ("slab", "row")
HIGHEST = lax.Precision.HIGHEST
STEP = 2
PANEL = 8
QUARTER = 160
VMEM_LIMIT = 48 * 1024 * 1024


def coords(i):
    zh, c, y, x, zl = i & 1, (i >> 1) & 1, (i >> 2) & 3, (i >> 4) & 3, (i >> 6) & 3
    return {"x": x, "y": y, "z": zh * 4 + zl, "c": c}


def flat(d):
    zh, zl = d["z"] >> 2, d["z"] & 3
    return (((zl * 4 + d["x"]) * 4 + d["y"]) * 2 + d["c"]) * 2 + zh


def partner(x, axis, k):
    pairs = []
    for i in range(256):
        d = coords(i)
        d[axis] ^= k
        pairs.append((i, flat(d)))
    return lax.ppermute(x, AXES, pairs)


ROUNDS = (("c", (1,)), ("x", (1, 2, 3)), ("y", (1, 2, 3)), ("z", (1, 2, 3)), ("z", (4,)))


def all_sum(x, given=None, tasks=None):
    for n, (axis, ks) in enumerate(ROUNDS):
        task = (tasks or {}).get(n)
        if task is not None:
            x, given = lax.optimization_barrier((x, given))
            given = task(*given)
        for part in [partner(x, axis, k) for k in ks]:
            x = x + part
        if task is not None:
            x, given = lax.optimization_barrier((x, given))
    return (x, given) if tasks else x


def x_coord():
    return (lax.axis_index("slab") >> 3) & 3


def all_sum_quarters(quarters):
    own = quarters[0]
    for part in [partner(quarters[k], "x", k) for k in (1, 2, 3)]:
        own = own + part
    for axis, ks in ROUNDS:
        if axis != "x":
            for part in [partner(own, axis, k) for k in ks]:
                own = own + part
    return [own] + [partner(own, "x", k) for k in (1, 2, 3)]


def exchange(edges):
    head, tail = edges
    count = lax.axis_size("slab") * lax.axis_size("row")
    low = lax.ppermute(tail, AXES, [(i, i + 1) for i in range(count - 1)])
    return low, lax.ppermute(head, AXES, [(i + 1, i) for i in range(count - 1)])


def split(x):
    hi = x.astype(jnp.bfloat16)
    return hi, (x - hi.astype(jnp.float32)).astype(jnp.bfloat16)


def dot3(a, b, dims):
    def dot(u, v):
        return lax.dot_general(u, v, (dims, ((), ())), preferred_element_type=jnp.float32)

    kept = 1 - dims[0][0]
    size = a[0].shape[kept]
    stacked = dot(jnp.concatenate(a, kept), b[0])
    return stacked[:size] + (dot(a[0], b[1]) + stacked[size:])


NT = ((1,), (1,))
TN = ((0,), (0,))
NN = ((1,), (0,))


def exact(a, b, dims=NN):
    return lax.dot_general(a, b, (dims, ((), ())), precision=HIGHEST, preferred_element_type=jnp.float32)


def sym(a):
    return 0.5 * (a + a.T)


def factor_inverses(mats):
    eye = (
        lax.broadcasted_iota(jnp.int32, (COLS, COLS), 0) == lax.broadcasted_iota(jnp.int32, (COLS, COLS), 1)
    ).astype(jnp.float32)
    work = [jnp.concatenate([a, eye], 1) for a in mats]
    done = [[] for _ in mats]
    for p in range(0, COLS, PANEL):
        left = COLS - p
        rows = lax.broadcasted_iota(jnp.int32, (left, 2 * COLS), 0)
        for n, w in enumerate(work):
            cols = [jnp.broadcast_to(w[:, p + k : p + k + 1], (left, 2 * COLS)) for k in range(PANEL)]
            for j in range(PANEL):
                factor = jnp.where(rows > j, cols[j] * (1.0 / cols[j][j : j + 1, :]), 0.0)
                for k in range(j + 1, PANEL):
                    cols[k] = cols[k] - factor * cols[k][j : j + 1, :]
                w = w - factor * w[j : j + 1, :]
            done[n].append(w[:PANEL])
            work[n] = w[PANEL:]
    out = []
    for parts in done:
        w = jnp.concatenate(parts, 0)
        d = jnp.sum(w[:, :COLS] * eye, axis=1, keepdims=True)
        r = lax.rsqrt(d)
        r = r * (1.5 - 0.5 * d * r * r)
        out.append(w[:, COLS:] * r)
    return out


def first_parts(first):
    return (
        (sym(first[0:64, 0:64]), first[64:128, 0:64], sym(first[128:192, 0:64])),
        (sym(first[0:64, 64:128]), first[64:128, 64:128], sym(first[128:192, 64:128])),
    )


def halves(first, second):
    out = []
    for n, (xx, px, pp) in enumerate(first_parts(first)):
        sx, sp = second[64 * n : 64 * n + 64, 0:64], second[64 * n : 64 * n + 64, 64:128]
        ss = sym(second[128:192, 64 * n : 64 * n + 64])
        out.append(
            jnp.concatenate(
                [
                    jnp.concatenate([xx, px.T, sx.T], 1),
                    jnp.concatenate([px, pp, sp.T], 1),
                    jnp.concatenate([sx, sp, ss], 1),
                ],
                0,
            )
        )
    return out


def prepare(first, l1, out_ref):
    (_, px_k, pp_k), (xx_m, px_m, _) = first_parts(first)
    y1 = exact(l1, xx_m)
    l21 = exact(px_k, l1, NT)
    (l2,) = factor_inverses([pp_k - exact(l21, l21, NT)])
    y2 = exact(l2, px_m - exact(l21, y1))
    for n, part in enumerate((l1, l2, l21, y1, y2)):
        out_ref[64 * n : 64 * n + 64] = part


def chain(first, second, ready, total_rows):
    l1, l2, l21, y1, y2 = (ready[64 * n : 64 * n + 64] for n in range(5))
    gram_k, gram_m = halves(first, second)
    sx_k, sp_k, ss_k, sx_m = gram_k[128:, 0:64], gram_k[128:, 64:128], gram_k[128:, 128:], gram_m[128:, 0:64]
    l31 = exact(sx_k, l1, NT)
    l32 = exact(sp_k - exact(l31, l21, NT), l2, NT)
    (l3,) = factor_inverses([ss_k - exact(l31, l31, NT) - exact(l32, l32, NT)])
    z3 = exact(l3, exact(l3, sx_m - exact(l31, y1) - exact(l32, y2)), TN)
    z2 = exact(l2, y2 - exact(l32, z3, TN), TN)
    z1 = exact(l1, y1 - exact(l21, z2, TN) - exact(l31, z3, TN), TN)
    coeffs = jnp.concatenate([z1, z2, z3], 0)
    norm = sym(exact(coeffs, exact(gram_m, coeffs), TN))
    (ln,) = factor_inverses([norm * (1.0 / total_rows)])
    return exact(coeffs, ln, NT), gram_k, gram_m


def both(mixing):
    return jnp.concatenate([mixing, jnp.concatenate([jnp.zeros((64, 64), jnp.float32), mixing[64:]], 0)], 1)


def block_row(t, g, col_ref, k_ref, m_ref, hi_ref, lo_ref):
    acc = None
    for j in range(NNZ):
        at = col_ref[g, j]
        w = split(jnp.concatenate([k_ref[t, j], m_ref[t, j]], 0))
        term = dot3((hi_ref[at], lo_ref[at]), w, NT)
        acc = term if acc is None else acc + term
    return acc


def fill(hi_ref, lo_ref, at, tiles):
    for b in range(tiles.shape[1] // BS):
        hi_ref[at + b], lo_ref[at + b] = split(tiles[:, b * BS : (b + 1) * BS])


def pair_steps(first, col_ref, xp_ref, k_ref, m_ref, kd_ref, md_ref, out, hi_ref, lo_ref, acc_ref):
    kv_ref, mv_ref, parts_ref = out
    for t in range(STEP):
        g = first + t
        at = slice(t * BS, (t + 1) * BS)
        acc = block_row(t, g, col_ref, k_ref, m_ref, hi_ref, lo_ref)
        tile = xp_ref[:, pl.ds(pl.multiple_of(g * BS, BS), BS)]
        kv = acc[:, :BS] + kd_ref[:, at] * tile
        mv = acc[:, BS:] + md_ref[:, at] * tile
        kv_ref[:, at] = kv
        mv_ref[:, at] = mv
        parts_ref[:, at] = jnp.concatenate([kv[0:64], mv[0:64]], 0) / kd_ref[:, at]
        acc_ref[...] += dot3(split(jnp.concatenate([kv, mv], 0)), (hi_ref[g + FACE], lo_ref[g + FACE]), NT)


def pair_inner(col_ref, xp_ref, k_ref, m_ref, kd_ref, md_ref, kv_ref, mv_ref, parts_ref, acc_ref, hi_ref, lo_ref):
    i = pl.program_id(0)

    @pl.when(i == 0)
    def _():
        acc_ref[...] = jnp.zeros_like(acc_ref)
        fill(hi_ref, lo_ref, FACE, xp_ref[...])

    out = (kv_ref, mv_ref, parts_ref)
    pair_steps(i * STEP + FACE, col_ref, xp_ref, k_ref, m_ref, kd_ref, md_ref, out, hi_ref, lo_ref, acc_ref)


def fill_edges(v_ref, low_ref, high_ref, hi_ref, lo_ref):
    rows = v_ref.shape[1]
    blocks = rows // BS
    fill(hi_ref, lo_ref, 0, low_ref[...])
    fill(hi_ref, lo_ref, FACE, v_ref[:, : 2 * FACE * BS])
    fill(hi_ref, lo_ref, blocks - FACE, v_ref[:, rows - 2 * FACE * BS :])
    fill(hi_ref, lo_ref, FACE + blocks, high_ref[...])
    return blocks


def pair_edges(
    col_ref, xp_ref, low_ref, high_ref, part_ref, kvin_ref, mvin_ref, partsin_ref, k_ref, m_ref, kd_ref, md_ref,
    kv_ref, mv_ref, parts_ref, gram_ref, hi_ref, lo_ref, acc_ref,
):
    i = pl.program_id(0)

    @pl.when(i == 0)
    def _():
        acc_ref[...] = part_ref[...]
        fill_edges(xp_ref, low_ref, high_ref, hi_ref, lo_ref)

    first = i * (xp_ref.shape[1] // BS - FACE)
    out = (kv_ref, mv_ref, parts_ref)
    pair_steps(first, col_ref, xp_ref, k_ref, m_ref, kd_ref, md_ref, out, hi_ref, lo_ref, acc_ref)

    @pl.when(i == pl.num_programs(0) - 1)
    def _():
        gram = acc_ref[...]
        gram_ref[0:64] = jnp.concatenate([gram[0:64, 0:64], gram[128:192, 0:64]], 1)
        gram_ref[64:128] = jnp.concatenate([gram[64:128, 0:64], gram[192:256, 0:64]], 1)
        gram_ref[128:192] = jnp.concatenate([gram[64:128, 64:128], gram[192:256, 64:128]], 1)


def parts_steps(first, col_ref, xp_ref, parts_ref, k_ref, m_ref, kd_ref, md_ref, kv_ref, mv_ref, hi_ref, lo_ref, acc_ref):
    for t in range(STEP):
        g = first + t
        at = slice(t * BS, (t + 1) * BS)
        here = pl.ds(pl.multiple_of(g * BS, BS), BS)
        acc = block_row(t, g, col_ref, k_ref, m_ref, hi_ref, lo_ref)
        tile = parts_ref[:, here]
        kv = acc[:, :BS] + kd_ref[:, at] * tile
        mv = acc[:, BS:] + md_ref[:, at] * tile
        kv_ref[:, at] = kv
        mv_ref[:, at] = mv
        basis = tuple(jnp.concatenate([u, v[g + FACE]], 0) for u, v in zip(split(xp_ref[:, here]), (hi_ref, lo_ref)))
        acc_ref[...] += dot3(split(jnp.concatenate([kv, mv], 0)), basis, NT)


def parts_inner(col_ref, xp_ref, parts_ref, k_ref, m_ref, kd_ref, md_ref, kv_ref, mv_ref, acc_ref, hi_ref, lo_ref):
    i = pl.program_id(0)

    @pl.when(i == 0)
    def _():
        acc_ref[...] = jnp.zeros_like(acc_ref)
        fill(hi_ref, lo_ref, FACE, parts_ref[...])

    parts_steps(
        i * STEP + FACE, col_ref, xp_ref, parts_ref, k_ref, m_ref, kd_ref, md_ref, kv_ref, mv_ref, hi_ref, lo_ref, acc_ref
    )


def parts_edges(
    col_ref, at_ref, xp_ref, parts_ref, low_ref, high_ref, part_ref, gram_ref, kvin_ref, mvin_ref, k_ref, m_ref, kd_ref, md_ref,
    kv_ref, mv_ref, q0_ref, q1_ref, q2_ref, q3_ref, hi_ref, lo_ref, acc_ref, all_ref,
):
    i = pl.program_id(0)

    @pl.when(i == 0)
    def _():
        acc_ref[...] = part_ref[...]
        fill_edges(parts_ref, low_ref, high_ref, hi_ref, lo_ref)

    first = i * (xp_ref.shape[1] // BS - FACE)
    parts_steps(
        first, col_ref, xp_ref, parts_ref, k_ref, m_ref, kd_ref, md_ref, kv_ref, mv_ref, hi_ref, lo_ref, acc_ref
    )

    @pl.when(i == pl.num_programs(0) - 1)
    def _():
        gram = acc_ref[...]
        all_ref[0:192] = gram_ref[...]
        all_ref[192:448] = gram[:, 0:128]
        all_ref[448:512] = jnp.concatenate([gram[0:64, 128:192], gram[128:192, 128:192]], 1)
        all_ref[512:576] = jnp.concatenate([gram[64:128, 128:192], gram[192:256, 128:192]], 1)
        all_ref[576:640] = jnp.concatenate([gram[64:128, 192:256], gram[192:256, 192:256]], 1)
        for k, out in enumerate((q0_ref, q1_ref, q2_ref, q3_ref)):
            out[...] = all_ref[pl.ds(pl.multiple_of((at_ref[0] ^ k) * QUARTER, 8), QUARTER), :]


def search_steps(first, col_ref, xp_ref, s_ref, k_ref, m_ref, kd_ref, md_ref, hi_ref, lo_ref, acc_ref):
    for t in range(STEP):
        g = first + t
        at = slice(t * BS, (t + 1) * BS)
        here = pl.ds(pl.multiple_of(g * BS, BS), BS)
        acc = block_row(t, g, col_ref, k_ref, m_ref, hi_ref, lo_ref)
        s = s_ref[:, here]
        ks = acc[:, :BS] + kd_ref[:, at] * s
        ms = acc[:, BS:] + md_ref[:, at] * s
        basis = tuple(jnp.concatenate([u, v[g + FACE]], 0) for u, v in zip(split(xp_ref[:, here]), (hi_ref, lo_ref)))
        acc_ref[...] += dot3(split(jnp.concatenate([ks, ms], 0)), basis, NT)


def search_inner(col_ref, xp_ref, s_ref, k_ref, m_ref, kd_ref, md_ref, acc_ref, hi_ref, lo_ref):
    i = pl.program_id(0)

    @pl.when(i == 0)
    def _():
        acc_ref[...] = jnp.zeros_like(acc_ref)
        fill(hi_ref, lo_ref, FACE, s_ref[...])

    search_steps(i * STEP + FACE, col_ref, xp_ref, s_ref, k_ref, m_ref, kd_ref, md_ref, hi_ref, lo_ref, acc_ref)


def search_edges(col_ref, xp_ref, s_ref, low_ref, high_ref, part_ref, k_ref, m_ref, kd_ref, md_ref, gram_ref, hi_ref, lo_ref, acc_ref):
    i = pl.program_id(0)

    @pl.when(i == 0)
    def _():
        acc_ref[...] = part_ref[...]
        fill_edges(s_ref, low_ref, high_ref, hi_ref, lo_ref)

    first = i * (s_ref.shape[1] // BS - FACE)
    search_steps(first, col_ref, xp_ref, s_ref, k_ref, m_ref, kd_ref, md_ref, hi_ref, lo_ref, acc_ref)

    @pl.when(i == pl.num_programs(0) - 1)
    def _():
        gram = acc_ref[...]
        gram_ref[0:128] = gram[:, 0:128]
        gram_ref[128:192] = jnp.concatenate([gram[0:64, 128:192], gram[64:128, 128:192]], 1)


def factor_pair(first_ref, inv_ref, ready_ref):
    prepare(first_ref[...], inv_ref[...], ready_ref)


def next_first(first_ref, second_ref, pair_ref, firsto_ref, inv_ref):
    pair = pair_ref[...]
    gram_k, gram_m = halves(first_ref[...], second_ref[...])
    next_k = exact(pair, exact(gram_k, pair), TN)
    next_m = exact(pair, exact(gram_m, pair), TN)
    firsto_ref[0:64] = jnp.concatenate([next_k[0:64, 0:64], next_m[0:64, 0:64]], 1)
    firsto_ref[64:128] = jnp.concatenate([next_k[64:128, 0:64], next_m[64:128, 0:64]], 1)
    firsto_ref[128:192] = jnp.concatenate([next_k[64:128, 64:128], next_m[64:128, 64:128]], 1)
    (inv,) = factor_inverses([sym(next_k[0:64, 0:64])])
    inv_ref[...] = inv


def search_gram(both_parts, ritz):
    one = jnp.concatenate([both_parts[192:256], both_parts[320:384]], 1)
    two = jnp.concatenate([both_parts[256:320], both_parts[384:448]], 1)
    crossed = jnp.concatenate([both_parts[512:576], both_parts[576:640]], 1)
    old = one - exact(ritz, two, TN)
    crossed = exact(ritz, crossed, TN)
    own = []
    for n in range(2):
        at = slice(64 * n, 64 * n + 64)
        mixed = crossed[:, at]
        own.append(sym(both_parts[448:512, at]) - mixed - mixed.T + exact(crossed[:, 128 + 64 * n : 192 + 64 * n], ritz))
    return jnp.concatenate([old[:, 0:128], old[:, 128:256], jnp.concatenate(own, 1)], 0)


def second_search(
    total_rows, at_ref, q0_ref, q1_ref, q2_ref, q3_ref, kv_ref, mv_ref, ks_ref, ms_ref, kd_ref,
    s_ref, pair_ref, spread_ref, first_ref, second_ref, all_ref, ready_ref,
):
    for k, quarter in enumerate((q0_ref, q1_ref, q2_ref, q3_ref)):
        all_ref[pl.ds(pl.multiple_of((at_ref[0] ^ k) * QUARTER, 8), QUARTER), :] = quarter[...]
    first = all_ref[0:192]
    first_ref[...] = first
    (xx_k, _, _), (xx_m, _, _) = first_parts(first)
    inv, inv_k = factor_inverses([xx_m, xx_k])
    ritz = exact(inv, exact(inv, xx_k), TN)
    prepare(first, inv_k, ready_ref)
    second = search_gram(all_ref[...], ritz)
    second_ref[...] = second
    mixing, gram_k, _ = chain(first, second, ready_ref[...], total_rows)
    pair = both(mixing)
    pair_ref[...] = pair
    spread = jnp.concatenate([pair, -exact(ritz, pair[128:192])], 0)
    spread_ref[...] = spread
    new_ritz = sym(exact(mixing, exact(gram_k, mixing), TN)) * (1.0 / total_rows)
    weights = split(jnp.concatenate([spread[:, 0:64], -exact(spread[:, 0:64], new_ritz)], 0))
    for b in range(0, s_ref.shape[1], 512):
        at = slice(b, b + 512)
        parts = split(jnp.concatenate([kv_ref[:, at], ks_ref[:, at], mv_ref[:, at], ms_ref[:, at]], 0))
        s_ref[:, at] = dot3(weights, parts, TN) / kd_ref[:, at]


def mix(pair, xp_ref, s_ref, at):
    return dot3(pair, split(jnp.concatenate([xp_ref[:, at], s_ref[:, at]], 0)), TN)


def mix_pair(pair_ref, xp_ref, s_ref, xpo_ref):
    pair = split(pair_ref[...])
    for b in range(0, s_ref.shape[1], 512):
        at = slice(b, b + 512)
        xpo_ref[:, at] = mix(pair, xp_ref, s_ref, at)


def last_kernel(total_rows, first_ref, second_ref, ready_ref, xp_ref, s_ref, xo_ref, po_ref):
    mixing, _, _ = chain(first_ref[...], second_ref[...], ready_ref[...], total_rows)
    pair = split(both(mixing))
    for b in range(0, s_ref.shape[1], 512):
        at = slice(b, b + 512)
        new = mix(pair, xp_ref, s_ref, at)
        xo_ref[:, at] = new[0:64]
        po_ref[:, at] = new[64:128]


def whole():
    return pl.BlockSpec(memory_space=pltpu.VMEM)


def smem():
    return pl.BlockSpec(memory_space=pltpu.SMEM)


def anywhere():
    return pl.BlockSpec(memory_space=pl.ANY)


def f32(*shape):
    return jax.ShapeDtypeStruct(shape, jnp.float32)


def bf16_blocks(extended, rows):
    return [pltpu.VMEM((extended, rows, BS), jnp.bfloat16)] * 2


def call(kernel, name, ins, outs, shapes, scratch=(), grid=None, aliases=None, flops=0, moved=0):
    kwargs = {} if grid is None else {"grid": grid}
    return pl.pallas_call(
        kernel,
        in_specs=ins,
        out_specs=outs,
        out_shape=shapes,
        scratch_shapes=list(scratch),
        input_output_aliases=aliases or {},
        compiler_params=pltpu.CompilerParams(vmem_limit_bytes=VMEM_LIMIT),
        cost_estimate=pl.CostEstimate(flops=flops, bytes_accessed=moved, transcendentals=0),
        name=name,
        **kwargs,
    )


def shards(start_block, prior_direction, col_index, k_blocks, m_blocks, k_diagonal, m_diagonal):
    blocks = col_index.shape[0]
    rows = start_block.shape[1]
    devices = lax.axis_size("slab") * lax.axis_size("row")
    total_rows = float(rows * devices)
    edge = FACE * BS
    first_block = (lax.axis_index("slab") * lax.axis_size("row") + lax.axis_index("row")) * blocks - FACE
    col = col_index - first_block
    kd, md = k_diagonal[None, :], m_diagonal[None, :]
    inner, outer = ((blocks - 2 * FACE) // STEP,), (2,)
    last = blocks // STEP - 1
    extended = blocks + 2 * FACE

    def stored(at):
        blocked = pl.BlockSpec((STEP, NNZ, BS, BS), lambda i: (at(i), 0, 0, 0))
        return [blocked] * 2 + columns(1, at)

    def columns(height, at, count=2):
        return [pl.BlockSpec((height, STEP * BS), lambda i: (0, at(i)))] * count

    def inside(i):
        return i + 1

    def at_edge(i):
        return i * last

    def edges(v):
        return v[:, :edge], v[:, rows - edge :]

    big = {"flops": 3 * 2 * 2 * 128 * 384 * 256 * blocks, "moved": 8 * blocks * NNZ * BS * BS}
    matrices = (k_blocks, m_blocks, kd, md)

    xp = jnp.concatenate([start_block, prior_direction], 0)
    low, high = exchange(edges(xp))
    kv, mv, parts, part = call(
        pair_inner, "pair_inner",
        [smem(), whole()] + stored(inside),
        columns(128, inside, 3) + [whole()],
        [f32(128, rows)] * 3 + [f32(256, 128)],
        bf16_blocks(extended, 128), inner, **big,
    )(col, xp, *matrices)
    kv, mv, parts, gram = call(
        pair_edges, "pair_edges",
        [smem()] + [whole()] * 4 + [anywhere()] * 3 + stored(at_edge),
        columns(128, at_edge, 3) + [whole()],
        [f32(128, rows)] * 3 + [f32(192, 128)],
        bf16_blocks(extended, 128) + [pltpu.VMEM((256, 128), jnp.float32)], outer, {5: 0, 6: 1, 7: 2},
    )(col, xp, low, high, part, kv, mv, parts, *matrices)

    low, high = exchange(edges(parts))
    ks, ms, part = call(
        parts_inner, "parts_inner",
        [smem()] + [whole()] * 2 + stored(inside),
        columns(128, inside) + [whole()],
        [f32(128, rows), f32(128, rows), f32(256, 256)],
        bf16_blocks(extended, 128), inner, **big,
    )(col, xp, parts, *matrices)
    at = x_coord().astype(jnp.int32)[None]
    ks, ms, *quarters = call(
        parts_edges, "parts_edges",
        [smem()] * 2 + [whole()] * 6 + [anywhere()] * 2 + stored(at_edge),
        columns(128, at_edge) + [whole()] * 4,
        [f32(128, rows), f32(128, rows)] + [f32(QUARTER, 128)] * 4,
        bf16_blocks(extended, 128) + [pltpu.VMEM((256, 256), jnp.float32), pltpu.VMEM((4 * QUARTER, 128), jnp.float32)],
        outer, {8: 0, 9: 1},
    )(col, at, xp, parts, low, high, part, gram, ks, ms, *matrices)

    quarters = all_sum_quarters(quarters)

    new, pair, spread, first, second = call(
        lambda *refs: second_search(total_rows, *refs), "second_search",
        [smem()] + [whole()] * 9, [whole()] * 5,
        [f32(64, rows), f32(192, 128), f32(256, 128), f32(192, 128), f32(192, 128)],
        [pltpu.VMEM((4 * QUARTER, 128), jnp.float32), pltpu.VMEM((320, 64), jnp.float32)],
    )(at, *quarters, kv, mv, ks, ms, kd)

    def factor(first, inv):
        return first, call(factor_pair, "factor_pair", [whole()] * 2, whole(), f32(320, 64))(first, inv)

    def grams(first, second, pair):
        return call(
            next_first, "next_first", [whole()] * 3, [whole()] * 2, [f32(192, 128), f32(64, 64)]
        )(first, second, pair)

    low, high = exchange(edges(new))
    xp = call(mix_pair, "mix_pair", [whole()] * 3, whole(), f32(128, rows))(spread, xp, parts)
    (part,) = call(
        search_inner, "second_inner",
        [smem()] + [whole()] * 2 + stored(inside), [whole()], [f32(128, 192)],
        bf16_blocks(extended, 64), inner, **big,
    )(col, xp, new, *matrices)
    (gram,) = call(
        search_edges, "second_edges",
        [smem()] + [whole()] * 5 + stored(at_edge), [whole()], [f32(192, 128)],
        bf16_blocks(extended, 64) + [pltpu.VMEM((128, 192), jnp.float32)], outer,
    )(col, xp, new, low, high, part, *matrices)

    second, (first, ready) = all_sum(gram, (first, second, pair), {3: grams, 4: factor})

    iterate, prior = call(
        lambda *refs: last_kernel(total_rows, *refs), "last_mix",
        [whole()] * 5, [whole()] * 2, [f32(64, rows)] * 2,
    )(first, second, ready, xp, new)
    return (iterate, prior)


def solution(mesh):
    in_specs = (
        P(None, ("slab", "row")),
        P(None, ("slab", "row")),
        P(("slab", "row"), None),
        P(("slab", "row"), None, None, None),
        P(("slab", "row"), None, None, None),
        P(("slab", "row")),
        P(("slab", "row")),
    )
    out_specs = (P(None, ("slab", "row")), P(None, ("slab", "row")))
    return jax.shard_map(shards, mesh=mesh, in_specs=in_specs, out_specs=out_specs, check_vma=False)
```
